128 devices in a mesh: dp: 32 (over z, x, core), section: 4 (over y).
Axes of the slice: x: 4, y: 4, z: 4, core: 2. Of those that a mesh axis runs over, the one named last changes fastest.
Arguments:
- tokens: bfloat16 [64, 256, 768], P('dp'), may hold values from -6 to 6
- cotangent: bfloat16 [64, 256, 768], P('dp'), may hold values from -6 to 6
- page_numbers: int32 [64, 256], P('dp'), may hold values from 0 to 7, never falling along the last dimension, each value on 1 to 128 neighbouring positions
- offset_bucket: int32 [511], replicated, may hold values from 0 to 31
- attend_gain: float32 [2, 768], replicated, may hold values from 0.5 to 1.5
- attend_shift: float32 [2, 768], replicated, may hold values from -1.5 to 1.5
- input_weight: bfloat16 [2, 768, 2304], replicated, may hold values from -0.21875 to 0.21875
- query_bias: float32 [2, 768], replicated, may hold values from -1.5 to 1.5
- value_bias: float32 [2, 768], replicated, may hold values from -1.5 to 1.5
- bias_table: float32 [2, 12, 32], replicated, may hold values from -4 to 4
- output_weight: bfloat16 [2, 768, 768], replicated, may hold values from -0.625 to 0.625
- output_bias: float32 [2, 768], replicated, may hold values from -1.5 to 1.5
- attend_scale: float32 [2, 768], replicated, may hold values from 0.5 to 2
- forward_gain: float32 [2, 768], replicated, may hold values from 0.5 to 1.5
- forward_shift: float32 [2, 768], replicated, may hold values from -1.5 to 1.5
- upward_weight: bfloat16 [2, 768, 3072], replicated, may hold values from -0.21875 to 0.21875
- upward_bias: float32 [2, 3072], replicated, may hold values from -1.5 to 1.5
- downward_weight: bfloat16 [2, 3072, 768], replicated, may hold values from -0.109375 to 0.109375
- downward_bias: float32 [2, 768], replicated, may hold values from -1.5 to 1.5
- forward_scale: float32 [2, 768], replicated, may hold values from 0.5 to 2
Outputs:
- section_outputs: bfloat16 [4, 64, 256, 768], P('section', 'dp')
- input_gradients: bfloat16 [4, 64, 256, 768], P('section', 'dp')
- attend_gain_gradient: float32 [2, 768], P(None, 'dp')
- attend_shift_gradient: float32 [2, 768], P(None, 'dp')
- input_weight_gradient: float32 [2, 768, 2304], P(None, 'dp')
- query_bias_gradient: float32 [2, 768], P(None, 'dp')
- value_bias_gradient: float32 [2, 768], P(None, 'dp')
- bias_table_gradient: float32 [2, 12, 32], replicated
- output_weight_gradient: float32 [2, 768, 768], P(None, 'dp')
- output_bias_gradient: float32 [2, 768], P(None, 'dp')
- attend_scale_gradient: float32 [2, 768], P(None, 'dp')
- forward_gain_gradient: float32 [2, 768], P(None, 'dp')
- forward_shift_gradient: float32 [2, 768], P(None, 'dp')
- upward_weight_gradient: float32 [2, 768, 3072], P(None, 'dp')
- upward_bias_gradient: float32 [2, 3072], P(None, 'dp')
- downward_weight_gradient: float32 [2, 3072, 768], P(None, 'dp')
- downward_bias_gradient: float32 [2, 768], P(None, 'dp')
- forward_scale_gradient: float32 [2, 768], P(None, 'dp')
The draws below stay inside these ranges and needn't reach their ends.
Inputs may be any that keep to these rules, and one draw needn't show every extreme that they name: `page_numbers`: in each row page numbers never fall and take every value from 0 to 7; a page covers at most 128 positions.
All inputs are finite; a program needn't handle non-finite values.
Results may differ from the reference program's by a relative error of at most 0.017.
Values may be sent and summed in bfloat16 or wider, within the bound.
A program may use at most 256 MiB of HBM per device.

```python
import math
import jax
import jax.numpy as jnp
import numpy as np
from jax import lax

D = 768
H = 12
HD = 64
FF = 3072
NB = 32
MB = 256
PAGES = 8
BATCHES = 64
SPAN = 511
QROWS = 256


def set_ends(entries, rng, low, top_value):
    longest = entries.shape.index(max(entries.shape))
    spots = []
    for shift in (0, 1):
        where = [jax.random.randint(jax.random.fold_in(rng, axis), (), 0, length) for axis, length in enumerate(entries.shape)]
        where[longest] = (where[longest] + shift) % entries.shape[longest]
        spots.append(tuple(where))
    return entries.at[spots[0]].set(low).at[spots[1]].set(top_value)


def block_scale(rng, dims, cuts, least, high):
    loudness = 1.0
    for position, shards_of in cuts:
        steps = jax.random.uniform(jax.random.fold_in(jax.random.fold_in(rng, 6), position), (shards_of,), jnp.float32, least / len(cuts), high / len(cuts))
        loudness = loudness * jnp.repeat(jnp.exp(steps), dims[position] // shards_of).reshape((-1,) + (1,) * (len(dims) - 1 - position))
    return loudness


def split_up(number_of, total, reach, skew):
    loads = [(1 << 20) // math.isqrt(standing ** skew) + 1 for standing in range(2, number_of + 1)]
    rest, counts = total - reach - (number_of - 1), [1] * (number_of - 1)
    while rest > 0:
        movable = [i for i in range(number_of - 1) if counts[i] < reach]
        pool, budget = sum([loads[i] for i in movable]), rest
        for i in movable:
            extra = min(reach - counts[i], max(1, budget * loads[i] // pool), rest)
            counts[i] = counts[i] + extra
            rest = rest - extra
    return np.array([reach] + counts)


def ragged_sizes(stream_key, amount, total, bound, skew):
    if amount == 2:
        one = jax.random.randint(stream_key, (), max(1, total - bound), min(bound, total - 1) + 1)
        return jnp.stack([one, total - one])
    sizes = jnp.asarray(split_up(amount, total, bound, skew), jnp.int32)
    twos = (amount - 1) // 2
    source_of, receiver = sizes[1:1 + 2 * twos:2], sizes[2:2 + 2 * twos:2]
    slack = jnp.minimum(source_of - 1, bound - receiver)
    shifted = jax.random.randint(jax.random.fold_in(stream_key, 1), (twos,), 0, 1 << 20) % (slack + 1)
    sizes = sizes.at[1:1 + 2 * twos:2].set(source_of - shifted).at[2:2 + 2 * twos:2].set(receiver + shifted)
    return sizes[jax.random.permutation(jax.random.fold_in(stream_key, 2), amount)]


def noise(stream_key, dims, width, bound, cuts=(), kind=jnp.bfloat16):
    factor_of = block_scale(stream_key, dims, cuts, -0.22, 0.18) if cuts else 1.0
    drawn = jax.random.normal(stream_key, dims, jnp.float32) * width * factor_of
    return jnp.minimum(jnp.maximum(drawn, -bound), bound).astype(kind)


def setup_inputs(seed: int = 0) -> dict:
    keys = jax.random.split(jax.random.key(seed), 21)
    return {
        "tokens": noise(keys[0], (BATCHES, MB, D), 1.0, 6.0, ((0, 32),)),
        "cotangent": noise(keys[1], (BATCHES, MB, D), 1.0, 6.0, ((0, 32),)),
        "page_numbers": jax.vmap(lambda own: jnp.searchsorted(jnp.cumsum(ragged_sizes(own, PAGES, MB, MB // 2, 2)), jnp.arange(MB), side="right"))(jax.random.split(keys[2], BATCHES)).reshape((BATCHES, MB)).astype(jnp.int32),
        "offset_bucket": set_ends(jax.random.randint(keys[3], (SPAN,), 0, NB), jax.random.fold_in(keys[3], 1), 0, NB - 1).astype(jnp.int32),
        "attend_gain": jnp.clip(1.0 + 0.1 * jax.random.normal(keys[4], (2, D), jnp.float32), 0.5, 1.5),
        "attend_shift": noise(keys[5], (2, D), 0.3, 1.5, (), jnp.float32),
        "input_weight": noise(keys[6], (2, D, 3 * D), D ** -0.5, 0.21875),
        "query_bias": noise(keys[7], (2, D), 0.3, 1.5, (), jnp.float32),
        "value_bias": noise(keys[8], (2, D), 0.3, 1.5, (), jnp.float32),
        "bias_table": noise(keys[9], (2, H, NB), 1.0, 4.0, (), jnp.float32),
        "output_weight": noise(keys[10], (2, D, D), (D // 8) ** -0.5, 0.625),
        "output_bias": noise(keys[11], (2, D), 0.3, 1.5, (), jnp.float32),
        "attend_scale": jnp.clip(jnp.exp(jax.random.uniform(keys[12], (2, D), jnp.float32, math.log(0.5), math.log(2.0))), 0.5, 2.0),
        "forward_gain": jnp.clip(1.0 + 0.1 * jax.random.normal(keys[13], (2, D), jnp.float32), 0.5, 1.5),
        "forward_shift": noise(keys[14], (2, D), 0.3, 1.5, (), jnp.float32),
        "upward_weight": noise(keys[15], (2, D, FF), D ** -0.5, 0.21875),
        "upward_bias": noise(keys[16], (2, FF), 0.3, 1.5, (), jnp.float32),
        "downward_weight": noise(keys[17], (2, FF, D), FF ** -0.5, 0.109375),
        "downward_bias": noise(keys[18], (2, D), 0.3, 1.5, (), jnp.float32),
        "forward_scale": jnp.clip(jnp.exp(jax.random.uniform(keys[19], (2, D), jnp.float32, math.log(0.5), math.log(2.0))), 0.5, 2.0),
    }


@jax.custom_vjp
def low(v):
    return lax.optimization_barrier(v.astype(jnp.bfloat16)).astype(jnp.float32)

@jax.custom_vjp
def low_back(v):
    return v

def low_keep(v):
    return (low(v), None)

def low_pass(kept, grad):
    return (grad,)

def back_keep(v):
    return (v, None)

def back_low(kept, grad):
    return (low(grad),)
low.defvjp(low_keep, low_pass)
low_back.defvjp(back_keep, back_low)
EPSILON = 1e-05
NEGATIVE = -1e+30
HIGHEST = lax.Precision.HIGHEST

def normalize(hidden, gain, shift):
    center = hidden - lax.optimization_barrier(jnp.mean(hidden, axis=-1, keepdims=True))
    spread = lax.optimization_barrier(jnp.mean(center * center, axis=-1, keepdims=True))
    return center * lax.rsqrt(spread + EPSILON) * gain + shift

def attention(hidden, pages, offset_bias, gain, shift, input_weight, query_bias, value_bias, output_weight, output_bias):
    factor = HD ** (-0.5)
    lowered = low(normalize(hidden, gain, shift))
    project = jnp.dot(lowered, input_weight, precision=HIGHEST)
    queries = low_back(low(project[:, :D] + query_bias)).reshape(MB, H, HD)
    key_heads = low_back(low(project[:, D:2 * D])).reshape(MB, H, HD)
    value_heads = low_back(low(project[:, 2 * D:] + value_bias)).reshape(MB, H, HD)
    positions = jnp.arange(MB, dtype=jnp.int32)

    def block(start):
        rows = lax.dynamic_slice_in_dim(queries, start, QROWS, 0)
        row_positions = start + jnp.arange(QROWS, dtype=jnp.int32)
        offsets = (positions[None, :] - row_positions[:, None] + MB - 1).astype(jnp.int32)
        bias = jnp.take(offset_bias, offsets, axis=1)
        scores = jnp.einsum('qhd,khd->hqk', rows, key_heads, precision=HIGHEST) * factor + bias
        scores = low_back(scores)
        row_pages = lax.dynamic_slice_in_dim(pages, start, QROWS, 0)
        same = (row_pages[:, None] == pages[None, :])[None]
        scores = jnp.where(same, scores, NEGATIVE)
        top = lax.optimization_barrier(jnp.max(scores, axis=-1, keepdims=True))
        expo = jnp.exp(scores - top)
        probability = low(expo / lax.optimization_barrier(jnp.sum(expo, axis=-1, keepdims=True)))
        return jnp.einsum('hqk,khd->qhd', probability, value_heads, precision=HIGHEST)
    starts = (jnp.arange(MB // QROWS, dtype=jnp.int32) * QROWS).astype(jnp.int32)
    mixed = lax.map(jax.checkpoint(block), starts)
    mixed = low_back(low(mixed.reshape(MB, D)))
    return low_back(jnp.dot(mixed, output_weight, precision=HIGHEST) + output_bias)

def feed_forward(hidden, gain, shift, upward_weight, upward_bias, downward_weight, downward_bias):
    lowered = low(normalize(hidden, gain, shift))
    before = low_back(jnp.dot(lowered, upward_weight, precision=HIGHEST) + upward_bias)
    after = low(jax.nn.gelu(before, approximate=True))
    return low_back(jnp.dot(after, downward_weight, precision=HIGHEST) + downward_bias)

def forward(first_input, probes, params, pages, offset_bucket):
    attend_gain, attend_shift, input_weight, query_bias, value_bias, bias_table, output_weight, output_bias, attend_scale, forward_gain, forward_shift, upward_weight, upward_bias, downward_weight, downward_bias, forward_scale = params
    hidden = low_back(first_input + probes[0])
    results = []
    for section in range(4):
        layer = section // 2
        if section % 2 == 0:
            offset_bias = bias_table[layer][:, offset_bucket]
            branch = attention(hidden, pages, offset_bias, attend_gain[layer], attend_shift[layer], input_weight[layer], query_bias[layer], value_bias[layer], output_weight[layer], output_bias[layer])
            hidden = low(hidden + attend_scale[layer] * branch)
        else:
            branch = feed_forward(hidden, forward_gain[layer], forward_shift[layer], upward_weight[layer], upward_bias[layer], downward_weight[layer], downward_bias[layer])
            hidden = low(hidden + forward_scale[layer] * branch)
        if section < 3:
            hidden = low_back(hidden + probes[section + 1])
        results.append(hidden)
    return tuple(results)

def reference(tokens, cotangent, page_numbers, offset_bucket, attend_gain, attend_shift, input_weight, query_bias, value_bias, bias_table, output_weight, output_bias, attend_scale, forward_gain, forward_shift, upward_weight, upward_bias, downward_weight, downward_bias, forward_scale):
    params = tuple((array.astype(jnp.float32) for array in (attend_gain, attend_shift, input_weight, query_bias, value_bias, bias_table, output_weight, output_bias, attend_scale, forward_gain, forward_shift, upward_weight, upward_bias, downward_weight, downward_bias, forward_scale)))

    def one_batch(carry, item):
        first_row, back_row, pages = item
        probes = jnp.zeros((4, MB, D), jnp.float32)

        def wrapped(row_in, probe_in, param_in):
            return forward(row_in, probe_in, param_in, pages, offset_bucket)
        results, pullback = jax.vjp(wrapped, first_row.astype(jnp.float32), probes, params)
        zero = jnp.zeros((MB, D), jnp.float32)
        unused, probe_grad, param_grad = pullback((zero, zero, zero, back_row.astype(jnp.float32)))
        carry = jax.tree.map(lambda total, part: total + part, carry, param_grad)
        return (carry, (jnp.stack(results), probe_grad))
    start = jax.tree.map(jnp.zeros_like, params)
    totals, (outputs, gradients) = lax.scan(one_batch, start, (tokens, cotangent, page_numbers))
    section_outputs = jnp.transpose(outputs, (1, 0, 2, 3)).astype(jnp.bfloat16)
    input_gradients = jnp.transpose(gradients, (1, 0, 2, 3)).astype(jnp.bfloat16)
    return (section_outputs, input_gradients) + tuple(totals)
```

```python
import functools
import jax
import jax.numpy as jnp
from jax import lax
from jax.experimental import pallas as pl
from jax.experimental.pallas import tpu as pltpu
from jax.sharding import PartitionSpec as P

D, H, HD, FF, NB, MB = 768, 12, 64, 3072, 32, 256
R = 512
EPS = 1e-5
UF, UP, UL = 6, 6, 8
F32, BF16 = jnp.float32, jnp.bfloat16
C0 = 0.7978845608028654
C1 = 0.044715 * C0


def dot(a, b):
    return jnp.dot(a, b, preferred_element_type=F32)


def dot_rt(a, b):
    return lax.dot_general(a, b, (((1,), (1,)), ((), ())), preferred_element_type=F32)


def dot_lt(a, b):
    return lax.dot_general(a, b, (((0,), (0,)), ((), ())), preferred_element_type=F32)


def fold8(v):
    return jnp.sum(v.reshape(v.shape[0] // 8, 8, v.shape[1]), axis=0)


def rowsum(v):
    return jnp.sum(v, axis=0, keepdims=True)


def k1(yfun, tok, cot, pages, bucket, ag, ash, win, qb, vb, tab, wout, ob, asc, fg, fsh, wup, ub, wdn, db, fsc,
       so, go, parts, vec, e_st, af_st, dg_st,
       xs, low, qkv, E, mixed, br, af, dg, w_in, w_out, w_up, w_dn, T, cotv, gb, gm, glow, AB, vsc, Dsc, fch, ach,
       sem):
    y = yfun()
    def cp(src, dst, i):
        return pltpu.make_async_copy(src, dst, sem.at[i])
    def ldA(l):
        return [cp(win.at[l], w_in, 0), cp(wout.at[l], w_out, 1)]
    def ldF(l):
        return [cp(wup.at[l], w_up, 2), cp(wdn.at[l], w_dn, 3)]
    def start(cs):
        for c in cs: c.start()
    def wait(cs):
        for c in cs: c.wait()
    ctok = cp(tok, xs.at[0], 4)
    ccot = cp(cot, cotv, 5)
    ctok.start()
    start(ldA(0))
    start(ldF(0))
    ccot.start()
    lane = lax.broadcasted_iota(jnp.int32, (1, 128), 1)
    m0 = (lane < 64).astype(F32).astype(BF16)
    m1 = (lane >= 64).astype(F32).astype(BF16)
    lanef = lax.broadcasted_iota(jnp.int32, (MB, 128), 1).astype(F32)
    for mb in range(2):
        pf = jnp.broadcast_to(pages[mb:mb + 1, :].astype(F32), (128, MB)).T
        same = pf == lanef
        AB[0, mb] = jnp.where(same | (lanef > 7.5), 0.0, -1e30).astype(BF16)
        AB[1, mb] = jnp.where(same, 1.0, 0.0).astype(BF16)
    sel = (lax.broadcasted_iota(jnp.int32, (NB, 512), 0) == bucket[...]).astype(F32)

    def layernorm(s, gain, shift):
        def body(i, _):
            r = pl.ds(pl.multiple_of(i * 64, 64), 64)
            x = xs[s, r, :].astype(F32)
            c = x - jnp.mean(x, -1, keepdims=True)
            n = c * lax.rsqrt(jnp.mean(c * c, -1, keepdims=True) + EPS)
            low[s, r, :] = (n * gain + shift).astype(BF16)
            return 0
        lax.fori_loop(0, R // 64, body, 0, unroll=UL)

    def residual(s, val, bias, scale):
        b = val + bias
        br[s] = b.astype(BF16)
        xs[s + 1] = (xs[s].astype(F32) + scale * b).astype(BF16)

    def masks(g, mb, l):
        rows = pl.ds(pl.multiple_of(mb * MB, MB), MB)
        c = pl.multiple_of(g * 128, 128)
        q = qkv[l, rows, pl.ds(c, 128)]
        k = qkv[l, rows, pl.ds(D + c, 128)]
        v = qkv[l, rows, pl.ds(2 * D + c, 128)]
        km = jnp.concatenate([k * m0, k * m1], 0)
        vm = jnp.concatenate([v * m0, v * m1], 0)
        return rows, pl.ds(c, 128), q, km, vm

    def attn_fwd(l):
        s = 2 * l
        row = lambda ref: ref[pl.ds(l, 1), :]
        obias = lax.dot_general(tab[l], sel, (((1,), (0,)), ((), ())), precision=lax.Precision.HIGHEST, preferred_element_type=F32)
        def toep():
            base = [pltpu.roll(jnp.broadcast_to(obias[h:h + 1, :], (8, 512)), 257, 1, stride=1, stride_axis=0) for h in range(H)]
            base = jnp.concatenate(base, 0)
            for a in range(MB // 8):
                t = pltpu.roll(base, 8 * a, 1) if a else base
                for h in range(H):
                    T[h // 2, 8 * a:8 * a + 8, (h % 2) * MB:(h % 2) * MB + MB] = t[8 * h:8 * h + 8, :MB]
        with jax.named_scope('toep'):
            toep()
        layernorm(s, row(ag), row(ash))
        x = low[s]
        qkv[l, :, 0:D] = ((dot(x, w_in[:, 0:D]) + row(qb)) * 0.125).astype(BF16)
        qkv[l, :, D:2 * D] = dot(x, w_in[:, D:2 * D]).astype(BF16)
        qkv[l, :, 2 * D:3 * D] = (dot(x, w_in[:, 2 * D:3 * D]) + row(vb)).astype(BF16)
        def pair(it, _):
            mb, g = it // 6, it % 6
            rows, cols, q, km, vm = masks(g, mb, l)
            qx = jnp.concatenate([q, AB[0, mb]], 1)
            kx = jnp.concatenate([km, jnp.concatenate([AB[1, mb]] * 2, 0)], 1)
            sc = dot_rt(qx, kx) + T[g]
            s0, s1 = sc[:, :MB], sc[:, MB:]
            def soft(v):
                e = jnp.exp(v - jnp.max(v, -1, keepdims=True))
                return e * (1.0 / jnp.sum(e, -1, keepdims=True))
            e = jnp.concatenate([soft(s0), soft(s1)], 1).astype(BF16)
            E[it] = e
            mixed[l, rows, cols] = dot(e, vm).astype(BF16)
            return 0
        with jax.named_scope('pairs'):
            lax.fori_loop(0, 12, pair, 0, unroll=UP)
        residual(s, dot(mixed[l], w_out[...]), row(ob), row(asc))

    def ff_fwd(l):
        s = 2 * l + 1
        row = lambda ref: ref[pl.ds(l, 1), :]
        layernorm(s, row(fg), row(fsh))
        x = low[s]
        for j in range(4):
            u = dot(x, w_up[:, D * j:D * (j + 1)]) + ub[pl.ds(l, 1), D * j:D * (j + 1)]
            u2 = u * u
            t = jnp.tanh(u * (C0 + C1 * u2))
            h = 0.5 * t + 0.5
            af[:, D * j:D * (j + 1)] = (u * h).astype(BF16)
            dg[:, D * j:D * (j + 1)] = (h + (0.5 - 0.5 * t * t) * (u * (C0 + (3 * C1) * u2))).astype(BF16)
        residual(s, dot(af[...], w_dn[...]), row(db), row(fsc))

    def fwd(l, _):
        @pl.when(l == 1)
        def _():
            wait([cp(E, e_st, 6)])
        wait(ldA(l))
        attn_fwd(l)
        @pl.when(l == 0)
        def _():
            start(ldA(1))
            cp(E, e_st, 6).start()
        @pl.when(l == 1)
        def _():
            wait([cp(af, af_st, 7), cp(dg, dg_st, 8)])
        wait(ldF(l))
        ff_fwd(l)
        @pl.when(l == 0)
        def _():
            start(ldF(1))
            start([cp(af, af_st, 7), cp(dg, dg_st, 8)])
        return 0

    ctok.wait()
    lax.fori_loop(0, 2, fwd, 0)
    c_so = cp(xs.at[y + 1], so, 9)
    c_so.start()
    c_so.wait()
    ccot.wait()
    xs[4] = cotv[...]

    def head_back(s, scale):
        def body(i, c):
            a, b = c
            r = pl.ds(pl.multiple_of(i * 64, 64), 64)
            u = xs[s + 1, r, :].astype(F32)
            g = (u * scale).astype(BF16)
            gb[r, :] = g
            return a + fold8(u * br[s, r, :].astype(F32)), b + fold8(g.astype(F32))
        z = jnp.zeros((8, D), F32)
        a, b = lax.fori_loop(0, R // 64, body, (z, z), unroll=UL)
        return rowsum(a), rowsum(b)

    def tail_back(s, gain):
        def body(i, c):
            a, b = c
            r = pl.ds(pl.multiple_of(i * 64, 64), 64)
            x = xs[s, r, :].astype(F32)
            gl = glow[r, :]
            ce = x - jnp.mean(x, -1, keepdims=True)
            rs = lax.rsqrt(jnp.mean(ce * ce, -1, keepdims=True) + EPS)
            n = ce * rs
            gn = gl * n
            t = gl * gain
            u = xs[s + 1, r, :].astype(F32)
            o = u + rs * (t - jnp.mean(t, -1, keepdims=True) - n * jnp.mean(t * n, -1, keepdims=True))
            xs[s, r, :] = o.astype(BF16)
            return a + fold8(gn), b + fold8(gl)
        z = jnp.zeros((8, D), F32)
        a, b = lax.fori_loop(0, R // 64, body, (z, z), unroll=UL)
        return rowsum(a), rowsum(b)

    def put_rows(dst, b, val, nb):
        for o in range(16):
            zz, xx, cc = o // 8, (o // 2) % 4, o % 2
            rows = val[24 * o:24 * o + 24, :]
            chunk = jnp.concatenate([rows[:, 384 * k:384 * (k + 1)] for k in range(nb)], 0)
            dst[cc, 2 * b + zz, xx] = chunk.astype(BF16)

    def ff_bwd(l):
        s = 2 * l + 1
        row = lambda ref: ref[pl.ds(l, 1), :]
        v0 = l * 16
        sg, dbg = head_back(s, row(fsc))
        vsc[pl.ds(v0 + 9, 1), :] = sg
        vsc[pl.ds(v0 + 8, 1), :] = dbg
        g = gb[...]
        for j in range(4):
            c = slice(D * j, D * (j + 1))
            ga = dot_rt(g, w_dn[c, :])
            gbef = (ga * dg[:, c].astype(F32)).astype(BF16)
            dg[:, c] = gbef
            vsc[pl.ds(v0 + 10 + j, 1), :] = rowsum(fold8(gbef.astype(F32)))
        glow[...] = dot_rt(dg[...], w_up[...])
        @pl.when(y < 2)
        def _():
            def b2(b, _):
                a = low[s, :, pl.ds(pl.multiple_of(b * 384, 128), 384)]
                put_rows(fch, b, dot_lt(a, dg[:, pl.ds(pl.multiple_of(y * 1536, 128), 1536)]), 4)
                return 0
            lax.fori_loop(0, 2, b2, 0)
        @pl.when(y >= 2)
        def _():
            gq = gb[:, pl.ds(pl.multiple_of((y - 2) * 384, 128), 384)]
            def b4(zz, _):
                a = af[:, pl.ds(pl.multiple_of(zz * 768, 128), 768)]
                val = dot_lt(a, gq).astype(BF16)
                for o in range(8):
                    fch[o % 2, zz, o // 2] = val[96 * o:96 * o + 96, :]
                return 0
            lax.fori_loop(0, 4, b4, 0)
        gg, sh = tail_back(s, row(fg))
        vsc[pl.ds(v0 + 6, 1), :] = gg
        vsc[pl.ds(v0 + 7, 1), :] = sh
        c = cp(fch, parts.at[:, :, :, pl.ds(pl.multiple_of(96 * l, 96), 96), :], 9)
        c.start()
        c.wait()

    def attn_bwd(l):
        s = 2 * l
        row = lambda ref: ref[pl.ds(l, 1), :]
        v0 = l * 16
        sg, obg = head_back(s, row(asc))
        vsc[pl.ds(v0 + 5, 1), :] = sg
        vsc[pl.ds(v0 + 4, 1), :] = obg
        gm[...] = dot_rt(gb[...], w_out[...]).astype(BF16)
        def pair(it, _):
            mb, g = it // 6, it % 6
            rows, cols, q, km, vm = masks(g, mb, l)
            dop = gm[rows, cols]
            dp = dot_rt(dop, vm)
            e = E[it]
            ef = e.astype(F32)
            pt = ef * dp
            in0 = jnp.sum(pt[:, :MB], -1, keepdims=True) / jnp.sum(ef[:, :MB], -1, keepdims=True)
            in1 = jnp.sum(pt[:, MB:], -1, keepdims=True) / jnp.sum(ef[:, MB:], -1, keepdims=True)
            ds = jnp.concatenate([pt[:, :MB] - ef[:, :MB] * in0, pt[:, MB:] - ef[:, MB:] * in1], 1).astype(BF16)
            dsf = ds.astype(F32)
            @pl.when(mb == 0)
            def _():
                T[g] = dsf
            @pl.when(mb == 1)
            def _():
                T[g] = T[g] + dsf
            dv = dot_lt(e, dop)
            dk = dot_lt(ds, q)
            dq = dot(ds, km) * 0.125
            hm = lane < 64
            c0 = pl.multiple_of(g * 128, 128)
            qkv[l, rows, pl.ds(c0, 128)] = dq.astype(BF16)
            qkv[l, rows, pl.ds(D + c0, 128)] = jnp.where(hm, dk[:MB], dk[MB:]).astype(BF16)
            qkv[l, rows, pl.ds(2 * D + c0, 128)] = jnp.where(hm, dv[:MB], dv[MB:]).astype(BF16)
            return 0
        with jax.named_scope('pairs'):
            lax.fori_loop(0, 12, pair, 0, unroll=UP)
        def cs(i, c):
            a, b = c
            r = pl.ds(pl.multiple_of(i * 64, 64), 64)
            return a + fold8(qkv[l, r, 0:D].astype(F32)), b + fold8(qkv[l, r, 2 * D:3 * D].astype(F32))
        z = jnp.zeros((8, D), F32)
        a, b = lax.fori_loop(0, R // 64, cs, (z, z), unroll=UL)
        vsc[pl.ds(v0 + 2, 1), :] = rowsum(a)
        vsc[pl.ds(v0 + 3, 1), :] = rowsum(b)
        @pl.when(y < 3)
        def _():
            def b2(b, _):
                a = low[s, :, pl.ds(pl.multiple_of(b * 384, 128), 384)]
                put_rows(ach, b, dot_lt(a, qkv[l, :, pl.ds(pl.multiple_of(y * D, 128), D)]), 2)
                return 0
            lax.fori_loop(0, 2, b2, 0)
        @pl.when(y == 3)
        def _():
            def b2(b, _):
                a = mixed[l, :, pl.ds(pl.multiple_of(b * 384, 128), 384)]
                put_rows(ach, b, dot_lt(a, gb[...]), 2)
                return 0
            lax.fori_loop(0, 2, b2, 0)
        glow[...] = dot_rt(qkv[l], w_in[...])
        gg, sh = tail_back(s, row(ag))
        vsc[pl.ds(v0 + 0, 1), :] = gg
        vsc[pl.ds(v0 + 1, 1), :] = sh
        def fo(h, _):
            a = T[h // 2, :, pl.ds(pl.multiple_of((h % 2) * MB, MB), MB)]
            a = jnp.concatenate([a, jnp.zeros((MB, MB), F32)], 1)
            n = MB // 2
            while n >= 1:
                a = a[n:, :] + pltpu.roll(a[:n, :], n, 1)
                n //= 2
            Dsc[pl.ds(h, 1), :] = a
            return 0
        with jax.named_scope('fold'):
            lax.fori_loop(0, H, fo, 0, unroll=UF)
        tg = lax.dot_general(Dsc[...], sel, (((1,), (1,)), ((), ())), precision=lax.Precision.HIGHEST, preferred_element_type=F32)
        vsc[32:48, pl.ds(pl.multiple_of(l * 128, 128), 128)] = jnp.concatenate([tg, jnp.zeros((16, 96), F32)], 1)
        c = cp(ach, parts.at[:, :, :, pl.ds(pl.multiple_of(192 + 48 * l, 48), 48), :], 9)
        c.start()
        c.wait()

    vsc[...] = jnp.zeros_like(vsc)
    Dsc[...] = jnp.zeros_like(Dsc)

    def bwd(i, _):
        l = 1 - i
        @pl.when(l == 0)
        def _():
            wait(ldF(0))
            wait([cp(af_st, af, 7), cp(dg_st, dg, 8)])
        ff_bwd(l)
        @pl.when(l == 1)
        def _():
            start(ldF(0))
            start([cp(af_st, af, 7), cp(dg_st, dg, 8)])
        @pl.when(l == 0)
        def _():
            wait(ldA(0))
            wait([cp(e_st, E, 6)])
        attn_bwd(l)
        @pl.when(l == 1)
        def _():
            start(ldA(0))
            cp(e_st, E, 6).start()
        return 0
    lax.fori_loop(0, 2, bwd, 0)
    c_go = cp(xs.at[y], go, 9)
    c_go.start()
    c_v = cp(vsc, vec, 10)
    c_v.start()
    c_go.wait()
    c_v.wait()


def run_k1(yfun, tokens, cotangent, pages, bucket, ag, ash, win, qb, vb, tab, wout, ob, asc, fg, fsh, wup, ub, wdn, db, fsc):
    tok = tokens.reshape(R, D)
    cot = cotangent.reshape(R, D)
    bucket = jnp.pad(bucket, (0, 1), constant_values=-1).reshape(1, 512)
    ANY = pl.BlockSpec(memory_space=pl.ANY)
    V = pl.BlockSpec(memory_space=pltpu.VMEM)
    sds = jax.ShapeDtypeStruct
    outs = (sds((R, D), BF16), sds((R, D), BF16), sds((2, 4, 4, 288, 384), BF16), sds((48, D), F32),
            sds((12, MB, 512), BF16), sds((R, FF), BF16), sds((R, FF), BF16))
    vm = pltpu.VMEM
    scratch = [
        vm((5, R, D), BF16), vm((4, R, D), BF16), vm((2, R, 3 * D), BF16), vm((12, MB, 512), BF16),
        vm((2, R, D), BF16), vm((4, R, D), BF16), vm((R, FF), BF16), vm((R, FF), BF16),
        vm((D, 3 * D), BF16), vm((D, D), BF16), vm((D, FF), BF16), vm((FF, D), BF16),
        vm((6, MB, 512), F32), vm((R, D), BF16), vm((R, D), BF16), vm((R, D), BF16), vm((R, D), F32),
        vm((2, 2, MB, 128), BF16), vm((48, D), F32), vm((16, 512), F32), vm((2, 4, 4, 96, 384), BF16), vm((2, 4, 4, 48, 384), BF16),
        pltpu.SemaphoreType.DMA((11,)),
    ]
    return pl.pallas_call(
        functools.partial(k1, yfun),
        out_shape=outs,
        in_specs=[ANY, ANY, V, V, V, V, ANY, V, V, V, ANY, V, V, V, V, ANY, V, ANY, V, V],
        out_specs=(ANY,) * 7,
        scratch_shapes=scratch,
        compiler_params=pltpu.CompilerParams(vmem_limit_bytes=63400000),
        name="chain",
    )(tok, cot, pages, bucket, ag, ash, win, qb, vb, tab, wout, ob, asc, fg, fsh, wup, ub, wdn, db, fsc)


MESH = pl.DeviceIdType.MESH
UNITS = ((96, 96, 48), (240, 48, 32), (0, 96, 48), (192, 48, 16))


class Comm:
    def __init__(self, vec, s1, rc, rx1, rx2, s2, fin, G, vx, sems, semr, vsems, vsemr):
        d = lax.axis_index("dp")
        self.y = lax.axis_index("section")
        self.z, self.x, self.c = d // 8, (d // 2) % 4, d % 2
        self.vec, self.s1, self.rc, self.rx1, self.rx2, self.s2, self.fin, self.G, self.vx = vec, s1, rc, rx1, rx2, s2, fin, G, vx
        self.sems, self.semr, self.vsems, self.vsemr = sems, semr, vsems, vsemr

    def dev(self, z=None, x=None, c=None, y=None):
        z = self.z if z is None else z
        x = self.x if x is None else x
        c = self.c if c is None else c
        y = self.y if y is None else y
        return (z * 8 + x * 2 + c, y)

    def others(self, axis):
        me = getattr(self, axis)
        if axis == "c":
            return [1 - me]
        return [lax.rem(me + i, 4) for i in (2, 1, 3)]

    def barrier(self):
        b = pltpu.get_barrier_semaphore()
        for axis in "cxzy":
            for o in self.others(axis):
                pl.semaphore_signal(b, inc=1, device_id=self.dev(**{axis: o}), device_id_type=MESH)
        pl.semaphore_wait(b, 10)

    def copy(self, src, dst, s, r, device):
        return pltpu.make_async_remote_copy(src_ref=src, dst_ref=dst, send_sem=s, recv_sem=r, device_id=device, device_id_type=MESH)

    def halves(self, u):
        r0, n, a = UNITS[u]
        return (("x", "z", r0, a, 0), ("z", "x", r0 + a, n - a, 1))

    def c_copy(self, u, src):
        r0, n, _ = UNITS[u]
        o = 1 - self.c
        return self.copy(src, self.rc.at[:, :, r0:r0 + n, :], self.sems.at[u, 0, 0, 0], self.semr.at[u, 0, 0, 0], self.dev(c=o))

    def s1_src(self, axis, o, rows):
        return self.s1.at[:, o, rows, :] if axis == "x" else self.s1.at[o, :, rows, :]

    def s1_copy(self, u, half, o, slot):
        axis, _, r0, n, h = half
        rows = slice(r0, r0 + n)
        return self.copy(self.s1_src(axis, o, rows), self.rx1.at[slot, :, rows, :], self.sems.at[u, 1, h, o], self.semr.at[u, 1, h, slot],
                         self.dev(**{axis: o}))

    def s1_start(self, u, c_done):
        c_done()
        r0, n, _ = UNITS[u]

        def add(i, _):
            z, x = i // 4, i % 4
            self.s1[z, x, r0:r0 + n, :] = (self.s1[z, x, r0:r0 + n, :].astype(F32) + self.rc[z, x, r0:r0 + n, :].astype(F32)).astype(BF16)
            return 0
        lax.fori_loop(0, 16, add, 0)
        for half in self.halves(u):
            for o in self.others(half[0]):
                self.s1_copy(u, half, o, getattr(self, half[0])).start()

    def s2_copy(self, u, half, o, slot):
        _, axis, r0, n, h = half
        rows = slice(r0, r0 + n)
        return self.copy(self.s2.at[o, rows, :], self.rx2.at[slot, rows, :], self.sems.at[u, 2, h, o], self.semr.at[u, 2, h, slot],
                         self.dev(**{axis: o}))

    def s2_start(self, u):
        for half in self.halves(u):
            axis, axis2, r0, n, h = half
            me = getattr(self, axis)
            rows = slice(r0, r0 + n)
            for o in self.others(axis):
                self.s1_copy(u, half, o, o).wait_recv()

            def add(i, _):
                own = self.s1[i, me, rows, :] if axis == "x" else self.s1[me, i, rows, :]
                v = own.astype(F32)
                for o in self.others(axis):
                    v = v + self.rx1[o, i, rows, :].astype(F32)
                self.s2[i, rows, :] = v.astype(BF16)
                return 0
            lax.fori_loop(0, 4, add, 0)
            for o in self.others(axis2):
                self.s2_copy(u, half, o, getattr(self, axis2)).start()

    def y_copy(self, u, o, slot):
        r0, n, _ = UNITS[u]
        rows = slice(r0, r0 + n)
        return self.copy(self.fin.at[rows, :], self.G.at[slot, rows, :], self.sems.at[u, 3, 0, o], self.semr.at[u, 3, 0, slot], self.dev(y=o))

    def y_start(self, u):
        for half in self.halves(u):
            axis, axis2, r0, n, h = half
            me = getattr(self, axis2)
            rows = slice(r0, r0 + n)
            for o in self.others(axis2):
                self.s2_copy(u, half, o, o).wait_recv()
            v = self.s2[me, rows, :].astype(F32)
            for o in self.others(axis2):
                v = v + self.rx2[o, rows, :].astype(F32)
            v = v.astype(BF16)
            self.fin[rows, :] = v
            self.G[self.y, rows, :] = v
        for o in self.others("y"):
            self.y_copy(u, o, self.y).start()

    def y_done(self, u):
        for o in self.others("y"):
            self.y_copy(u, o, o).wait_recv()

    def sends_done(self, u, c_send):
        c_send()
        for half in self.halves(u):
            for o in self.others(half[0]):
                self.s1_copy(u, half, o, getattr(self, half[0])).wait_send()
            for o in self.others(half[1]):
                self.s2_copy(u, half, o, getattr(self, half[1])).wait_send()
        for o in self.others("y"):
            self.y_copy(u, o, self.y).wait_send()

    def v_copy(self, stage, axis, o, slot):
        return self.copy(self.vec, self.vx.at[stage, slot], self.vsems.at[stage, o], self.vsemr.at[stage, slot], self.dev(**{axis: o}))

    def v_start(self, stage):
        axis = "cxz"[stage]
        me = getattr(self, axis)
        for o in self.others(axis):
            self.v_copy(stage, axis, o, me).start()

    def v_finish(self, stage):
        axis = "cxz"[stage]
        me = getattr(self, axis)
        for o in self.others(axis):
            self.v_copy(stage, axis, o, o).wait_recv()
        for o in self.others(axis):
            self.v_copy(stage, axis, o, me).wait_send()
        self.vx[stage, me] = self.vec[...]
        v = self.vx[stage, 0] + self.vx[stage, 1]
        if stage:
            v = (v + self.vx[stage, 2]) + self.vx[stage, 3]
        self.vec[...] = v


def k2(parts, vec_in, G, vec, s1, rc, rx1, rx2, s2, fin, vx, lsem, sems, semr, vsems, vsemr):
    cm = Comm(vec, s1, rc, rx1, rx2, s2, fin, G, vx, sems, semr, vsems, vsemr)
    vec[...] = vec_in[...]
    locals_ = []
    for u, (r0, n, _) in enumerate(UNITS):
        locals_.append(pltpu.make_async_copy(parts.at[cm.c, :, :, r0:r0 + n, :], s1.at[:, :, r0:r0 + n, :], lsem.at[u]))
    for l in locals_:
        l.start()
    cm.barrier()
    csends = [cm.c_copy(u, parts.at[1 - cm.c, :, :, r0:r0 + n, :]) for u, (r0, n, _) in enumerate(UNITS)]
    cm.v_start(0)
    for c in csends:
        c.start()
    cm.v_finish(0)
    cm.v_start(1)
    for u in range(4):
        def c_done():
            locals_[u].wait()
            csends[u].wait_recv()
        cm.s1_start(u, c_done)
    cm.v_finish(1)
    cm.v_start(2)
    for u in range(4):
        cm.s2_start(u)
    for u in range(4):
        cm.y_start(u)
    cm.v_finish(2)
    for u in range(4):
        cm.y_done(u)
    for u in range(4):
        cm.sends_done(u, csends[u].wait_send)


def comm_scratch():
    vm = pltpu.VMEM
    return [vm((4, 4, 288, 384), BF16), vm((4, 4, 288, 384), BF16), vm((4, 4, 288, 384), BF16), vm((4, 288, 384), BF16),
            vm((4, 288, 384), BF16), vm((288, 384), BF16), vm((3, 4, 48, D), F32)]


def comm_sems():
    S = pltpu.SemaphoreType.DMA
    return [S((4, 4, 2, 4)), S((4, 4, 2, 4)), S((3, 4)), S((3, 4))]


def run_k2(parts, vec):
    V = pl.BlockSpec(memory_space=pltpu.VMEM)
    ANY = pl.BlockSpec(memory_space=pl.ANY)
    sds = jax.ShapeDtypeStruct
    return pl.pallas_call(
        k2,
        out_shape=(sds((4, 288, 384), BF16), sds((48, D), F32)),
        in_specs=[ANY, V],
        out_specs=(V, V),
        scratch_shapes=comm_scratch() + [pltpu.SemaphoreType.DMA((4,))] + comm_sems(),
        compiler_params=pltpu.CompilerParams(vmem_limit_bytes=48 << 20, collective_id=0, has_side_effects=True),
        name="reduce",
    )(parts, vec)


VEC_ROWS = (0, 1, 2, 3, 4, 5, 6, 7, 8, 9)


def k3(G, vec, a_gain, a_shift, w_in, qb, vb, tab, w_out, ob, asc, fg, fsh, w_up, ub, w_dn, db, fsc):
    d = lax.axis_index("dp")
    for l in range(2):
        for y in range(4):
            f = G[y, 96 * l:96 * l + 96, :].astype(F32)
            a = G[y, 192 + 48 * l:240 + 48 * l, :].astype(F32)
            if y < 2:
                for k in range(4):
                    w_up[l, :, 1536 * y + 384 * k:1536 * y + 384 * (k + 1)] = f[24 * k:24 * k + 24]
            else:
                w_dn[l, :, 384 * (y - 2):384 * (y - 1)] = f
            for k in range(2):
                if y < 3:
                    w_in[l, :, 768 * y + 384 * k:768 * y + 384 * (k + 1)] = a[24 * k:24 * k + 24]
                else:
                    w_out[l, :, 384 * k:384 * (k + 1)] = a[24 * k:24 * k + 24]
        r = pltpu.roll(vec[16 * l:16 * l + 16, :], lax.rem(D - 24 * d, D), 1)[:, :128]
        for ref, i in ((a_gain, 0), (a_shift, 1), (qb, 2), (vb, 3), (ob, 4), (asc, 5), (fg, 6), (fsh, 7), (db, 8), (fsc, 9)):
            ref[l:l + 1, :] = r[i:i + 1, :24]
        row = vec[pl.ds(16 * l + 10 + d // 8, 1), :]
        ub[l:l + 1, :] = pltpu.roll(jnp.broadcast_to(row, (8, D)), lax.rem(D - 96 * lax.rem(d, 8), D), 1)[0:1, :96]
        tab[l] = vec[32:32 + H, 128 * l:128 * l + NB]


def run_k3(G, vec):
    V = pl.BlockSpec(memory_space=pltpu.VMEM)
    sds = jax.ShapeDtypeStruct
    w = sds((2, 24), F32)
    outs = (w, w, sds((2, 24, 2304), F32), w, w, sds((2, H, NB), F32), sds((2, 24, D), F32), w, w, w, w, sds((2, 24, FF), F32), sds((2, 96), F32),
            sds((2, 96, D), F32), w, w)
    return pl.pallas_call(k3, out_shape=outs, in_specs=[V, V], out_specs=(V,) * 16, name="unpack",
                          compiler_params=pltpu.CompilerParams(vmem_limit_bytes=32 << 20))(G, vec)


def body(*args):
    so, go, parts, vec = run_k1(lambda: lax.axis_index("section"), *args)[:4]
    G, v = run_k2(parts, vec)
    return (so.reshape(1, 2, MB, D), go.reshape(1, 2, MB, D)) + tuple(run_k3(G, v))


def solution(mesh):
    data, whole = P("dp", None, None), P()
    w1, w2 = P(None, "dp"), P(None, "dp", None)
    return jax.shard_map(
        body,
        mesh=mesh,
        in_specs=(data, data, P("dp", None)) + (whole,) * 17,
        out_specs=(P("section", "dp", None, None),) * 2 + (w1, w1, w2, w1, w1, P(), w2, w1, w1, w1, w1, w2, w1, w2, w1, w1),
        check_vma=False,
    )
```

```python
import functools
import jax
import jax.numpy as jnp
from jax import lax
from jax.experimental import pallas as pl
from jax.experimental.pallas import tpu as pltpu
from jax.sharding import PartitionSpec as P

D, H, HD, FF, NB, MB = 768, 12, 64, 3072, 32, 256
R = 512
EPS = 1e-5
UF, UP, UL = 6, 6, 8
F32, BF16 = jnp.float32, jnp.bfloat16
C0 = 0.7978845608028654
C1 = 0.044715 * C0


def dot(a, b):
    return jnp.dot(a, b, preferred_element_type=F32)


def dot_rt(a, b):
    return lax.dot_general(a, b, (((1,), (1,)), ((), ())), preferred_element_type=F32)


def dot_lt(a, b):
    return lax.dot_general(a, b, (((0,), (0,)), ((), ())), preferred_element_type=F32)


def fold8(v):
    return jnp.sum(v.reshape(v.shape[0] // 8, 8, v.shape[1]), axis=0)


def rowsum(v):
    return jnp.sum(v, axis=0, keepdims=True)


MESH = pl.DeviceIdType.MESH
KINDS = ((96, 48, 0, 0), (48, 32, 192, 96))


class Comm:
    def __init__(self, vec, fch, ach, rc, rx1, rx2, s2, G, vx, sems, semr, vsems, vsemr, credit):
        d = lax.axis_index("dp")
        self.y = lax.axis_index("section")
        self.z, self.x, self.c = d // 8, lax.rem(d // 2, 4), lax.rem(d, 2)
        self.vec, self.own, self.rc, self.rx1, self.rx2, self.s2, self.G, self.vx = vec, (fch, ach), rc, rx1, rx2, s2, G, vx
        self.sems, self.semr, self.vsems, self.vsemr, self.credit = sems, semr, vsems, vsemr, credit

    def dev(self, axis, o):
        at = {"z": self.z, "x": self.x, "c": self.c, "y": self.y}
        at[axis] = o
        return (at["z"] * 8 + at["x"] * 2 + at["c"], at["y"])

    def others(self, axis):
        me = getattr(self, axis)
        if axis == "c":
            return [(1 - me, 0, 0)]
        return [(lax.rem(me + i, 4), 3 - i, i - 1) for i in (2, 1, 3)]

    def signal_all(self):
        b = pltpu.get_barrier_semaphore()
        for axis in "cxzy":
            for o, _, _ in self.others(axis):
                pl.semaphore_signal(b, inc=1, device_id=self.dev(axis, o), device_id_type=MESH)

    def wait_all(self):
        pl.semaphore_wait(pltpu.get_barrier_semaphore(), 10)

    def copy(self, src, dst, s, r, device):
        return pltpu.make_async_remote_copy(src_ref=src, dst_ref=dst, send_sem=s, recv_sem=r, device_id=device, device_id_type=MESH)

    def rows(self, kind, l, h=None):
        n, a, g, _ = KINDS[kind]
        base = g + n * l
        lo, m = (0, n) if h is None else ((0, a) if h == 0 else (a, n - a))
        return pl.ds(lo, m), pl.ds(pl.multiple_of(base + lo, 16), m)

    def unit(self, kind, l):
        return 2 * (1 - l) + kind

    def c_copy(self, kind, l):
        n, _, _, r = KINDS[kind]
        u = self.unit(kind, l)
        o = 1 - self.c
        return self.copy(self.own[kind].at[o], self.rc.at[:, :, r:r + n, :], self.sems.at[u, 0, 0, 0], self.semr.at[u, 0, 0, 0],
                         self.dev("c", o))

    def c_start(self, kind, l):
        if isinstance(l, int):
            if l == 0:
                pl.semaphore_wait(self.credit.at[kind], 1)
        else:
            @pl.when(l == 0)
            def _():
                pl.semaphore_wait(self.credit.at[kind], 1)
        self.c_copy(kind, l).start()

    def s1_copy(self, kind, l, h, o, there):
        axis = "xz"[h]
        u = self.unit(kind, l)
        mine, every = self.rows(kind, l, h)
        src = self.own[kind].at[self.c, :, o, mine, :] if axis == "x" else self.own[kind].at[self.c, o, :, mine, :]
        return self.copy(src, self.rx1.at[there, :, every, :], self.sems.at[u, 1, h, there], self.semr.at[u, 1, h, there], self.dev(axis, o))

    def s1_start(self, kind, l):
        n, _, _, r = KINDS[kind]
        own, c = self.own[kind], self.c
        cc = self.c_copy(kind, l)
        cc.wait_recv()

        def add(i, _):
            z, x = i // 4, lax.rem(i, 4)
            own[c, z, x] = (own[c, z, x].astype(F32) + self.rc[z, x, r:r + n, :].astype(F32)).astype(BF16)
            return 0
        lax.fori_loop(0, 16, add, 0)

        @pl.when(l == 1)
        def _():
            pl.semaphore_signal(self.credit.at[kind], inc=1, device_id=self.dev("c", 1 - c), device_id_type=MESH)
        for h in range(2):
            for o, there, _ in self.others("xz"[h]):
                self.s1_copy(kind, l, h, o, there).start()
        cc.wait_send()

    def s2_copy(self, kind, l, h, o, there):
        axis = "zx"[h]
        u = self.unit(kind, l)
        _, every = self.rows(kind, l, h)
        return self.copy(self.s2.at[o, every, :], self.rx2.at[there, every, :], self.sems.at[u, 2, h, there], self.semr.at[u, 2, h, there],
                         self.dev(axis, o))

    def s2_start(self, kind, l):
        own, c = self.own[kind], self.c
        for h in range(2):
            axis, axis2 = "xz"[h], "zx"[h]
            me = getattr(self, axis)
            mine, every = self.rows(kind, l, h)
            for o, _, here in self.others(axis):
                self.s1_copy(kind, l, h, o, here).wait_recv()

            def add(i, _):
                v = (own[c, i, me, mine, :] if axis == "x" else own[c, me, i, mine, :]).astype(F32)
                for k in range(3):
                    v = v + self.rx1[k, i, every, :].astype(F32)
                self.s2[i, every, :] = v.astype(BF16)
                return 0
            lax.fori_loop(0, 4, add, 0)
            for o, there, _ in self.others(axis2):
                self.s2_copy(kind, l, h, o, there).start()
            for o, there, _ in self.others(axis):
                self.s1_copy(kind, l, h, o, there).wait_send()

    def y_copy(self, kind, l, o, slot, there):
        u = self.unit(kind, l)
        _, every = self.rows(kind, l)
        part = self.G.at[slot, every, :]
        return self.copy(part, part, self.sems.at[u, 3, 0, there], self.semr.at[u, 3, 0, there], self.dev("y", o))

    def y_start(self, kind, l):
        for h in range(2):
            axis2 = "zx"[h]
            me = getattr(self, axis2)
            _, every = self.rows(kind, l, h)
            for o, _, here in self.others(axis2):
                self.s2_copy(kind, l, h, o, here).wait_recv()
            v = self.s2[me, every, :].astype(F32)
            for k in range(3):
                v = v + self.rx2[k, every, :].astype(F32)
            self.G[self.y, every, :] = v.astype(BF16)
            for o, there, _ in self.others(axis2):
                self.s2_copy(kind, l, h, o, there).wait_send()
        for o, there, _ in self.others("y"):
            self.y_copy(kind, l, o, self.y, there).start()

    def y_done(self, kind, l):
        for o, there, here in self.others("y"):
            self.y_copy(kind, l, o, o, here).wait_recv()
            self.y_copy(kind, l, o, self.y, there).wait_send()

    def v_copy(self, stage, o, there):
        i = (0, 1, 4)[stage] + there
        return self.copy(self.vec, self.vx.at[i], self.vsems.at[i], self.vsemr.at[i], self.dev("cxz"[stage], o))

    def v_start(self, stage):
        for o, there, _ in self.others("cxz"[stage]):
            self.v_copy(stage, o, there).start()

    def v_finish(self, stage):
        axis = "cxz"[stage]
        me = getattr(self, axis)
        for o, there, here in self.others(axis):
            self.v_copy(stage, o, here).wait_recv()
            self.v_copy(stage, o, there).wait_send()
        if stage == 0:
            self.vec[...] = self.vec[...] + self.vx[0]
            return
        own = self.vec[...]
        terms = []
        for p in range(4):
            slot = lax.rem(p - me + 7, 4)
            terms.append(jnp.where(slot == 3, own, self.vx[(1, 4)[stage - 1] + jnp.minimum(slot, 2)]))
        self.vec[...] = (terms[0] + terms[1]) + (terms[2] + terms[3])


def head_block(h):
    k = h % 6
    if isinstance(h, int):
        return h // 6, slice(MB * (k // 3), MB * (k // 3) + MB), slice(MB * (k % 3), MB * (k % 3) + MB)
    return h // 6, pl.ds(pl.multiple_of(MB * (k // 3), MB), MB), pl.ds(pl.multiple_of(MB * (k % 3), MB), MB)


def chain(tok, cot, pages, bucket, ag, ash, win, qb, vb, tab, wout, ob, asc, fg, fsh, wup, ub, wdn, db, fsc,
       so, go, G, vsc, e_st, af_st, dg_st,
       xs, low, qkv, E, mixed, br, af, dg, w_in, w_out, w_up, w_dn, T, AB, Dsc, bsc, fch, ach,
       rc, rx1, rx2, s2, vx, sem, sems, semr, vsems, vsemr, credit):
    cm = Comm(vsc, fch, ach, rc, rx1, rx2, s2, G, vx, sems, semr, vsems, vsemr, credit)
    y = cm.y
    def cp(src, dst, i):
        return pltpu.make_async_copy(src, dst, sem.at[i])
    def ldA(l):
        return [cp(win.at[l], w_in, 0), cp(wout.at[l], w_out, 1)]
    def ldF(l):
        return [cp(wup.at[l], w_up, 2), cp(wdn.at[l], w_dn, 3)]
    def start(cs):
        for c in cs: c.start()
    def wait(cs):
        for c in cs: c.wait()
    ctok = cp(tok, xs.at[0], 4)
    ccot = cp(cot, xs.at[5], 5)
    ctok.start()
    start(ldA(0))
    start(ldF(0))
    ccot.start()
    cm.signal_all()
    bsc[...] = jnp.full((1, 512), -1, jnp.int32)
    bsc[:, :511] = bucket[...]
    lane = lax.broadcasted_iota(jnp.int32, (1, 128), 1)
    m0 = (lane < 64).astype(F32).astype(BF16)
    m1 = (lane >= 64).astype(F32).astype(BF16)
    lanef = lax.broadcasted_iota(jnp.int32, (MB, 128), 1).astype(F32)
    for mb in range(2):
        pf = jnp.broadcast_to(pages[mb:mb + 1, :].astype(F32), (128, MB)).T
        same = pf == lanef
        AB[0, mb] = jnp.where(same | (lanef > 7.5), 0.0, -1e30).astype(BF16)
        AB[1, mb] = jnp.where(same, 1.0, 0.0).astype(BF16)
    sel = (lax.broadcasted_iota(jnp.int32, (NB, 512), 0) == bsc[...]).astype(F32)

    def layernorm(s, gain, shift):
        def body(i, _):
            r = pl.ds(pl.multiple_of(i * 64, 64), 64)
            x = xs[s, r, :].astype(F32)
            c = x - jnp.mean(x, -1, keepdims=True)
            n = c * lax.rsqrt(jnp.mean(c * c, -1, keepdims=True) + EPS)
            low[s, r, :] = (n * gain + shift).astype(BF16)
            return 0
        lax.fori_loop(0, R // 64, body, 0, unroll=UL)

    def residual(s, val, bias, scale):
        b = val + bias
        br[s] = b.astype(BF16)
        xs[s + 1] = (xs[s].astype(F32) + scale * b).astype(BF16)

    def masks(g, mb, l):
        rows = pl.ds(pl.multiple_of(mb * MB, MB), MB)
        c = pl.multiple_of(g * 128, 128)
        q = qkv[l, rows, pl.ds(c, 128)]
        k = qkv[l, rows, pl.ds(D + c, 128)]
        v = qkv[l, rows, pl.ds(2 * D + c, 128)]
        km = jnp.concatenate([k * m0, k * m1], 0)
        vm = jnp.concatenate([v * m0, v * m1], 0)
        return rows, pl.ds(c, 128), q, km, vm

    def attn_fwd(l):
        s = 2 * l
        row = lambda ref: ref[pl.ds(l, 1), :]
        obias = lax.dot_general(tab[:, pl.ds(l, 1), :].reshape(H, NB), sel, (((1,), (0,)), ((), ())), precision=lax.Precision.HIGHEST, preferred_element_type=F32)
        def toep():
            base = [pltpu.roll(jnp.broadcast_to(obias[h:h + 1, :], (8, 512)), 257, 1, stride=1, stride_axis=0) for h in range(H)]
            base = jnp.concatenate(base, 0)
            for a in range(MB // 8):
                t = pltpu.roll(base, 8 * a, 1) if a else base
                for h in range(H):
                    p, r, c = head_block(h)
                    T[p, r.start + 8 * a:r.start + 8 * a + 8, c] = t[8 * h:8 * h + 8, :MB]
        with jax.named_scope('toep'):
            toep()
        layernorm(s, row(ag), row(ash))
        x = low[s]
        qkv[l, :, 0:D] = ((dot(x, w_in[:, 0:D]) + row(qb)) * 0.125).astype(BF16)
        qkv[l, :, D:2 * D] = dot(x, w_in[:, D:2 * D]).astype(BF16)
        qkv[l, :, 2 * D:3 * D] = (dot(x, w_in[:, 2 * D:3 * D]) + row(vb)).astype(BF16)
        def pair(it, _):
            mb, g = it // 6, it % 6
            rows, cols, q, km, vm = masks(g, mb, l)
            qx = jnp.concatenate([q, AB[0, mb]], 1)
            kx = jnp.concatenate([km, jnp.concatenate([AB[1, mb]] * 2, 0)], 1)
            sc = dot_rt(qx, kx)
            s0, s1 = sc[:, :MB] + T[head_block(2 * g)], sc[:, MB:] + T[head_block(2 * g + 1)]
            def soft(v):
                e = jnp.exp(v - jnp.max(v, -1, keepdims=True))
                return e * (1.0 / jnp.sum(e, -1, keepdims=True))
            e = jnp.concatenate([soft(s0), soft(s1)], 1).astype(BF16)
            E[it] = e
            mixed[l, rows, cols] = dot(e, vm).astype(BF16)
            return 0
        with jax.named_scope('pairs'):
            lax.fori_loop(0, 12, pair, 0, unroll=UP)
        residual(s, dot(mixed[l], w_out[...]), row(ob), row(asc))

    def ff_fwd(l):
        s = 2 * l + 1
        row = lambda ref: ref[pl.ds(l, 1), :]
        layernorm(s, row(fg), row(fsh))
        x = low[s]
        for j in range(4):
            u = dot(x, w_up[:, D * j:D * (j + 1)]) + ub[pl.ds(l, 1), D * j:D * (j + 1)]
            u2 = u * u
            t = jnp.tanh(u * (C0 + C1 * u2))
            h = 0.5 * t + 0.5
            af[:, D * j:D * (j + 1)] = (u * h).astype(BF16)
            dg[:, D * j:D * (j + 1)] = (h + (0.5 - 0.5 * t * t) * (u * (C0 + (3 * C1) * u2))).astype(BF16)
        residual(s, dot(af[...], w_dn[...]), row(db), row(fsc))

    def fwd(l, _):
        @pl.when(l == 1)
        def _():
            wait([cp(E, e_st, 6)])
        wait(ldA(l))
        attn_fwd(l)
        @pl.when(l == 0)
        def _():
            start(ldA(1))
            cp(E, e_st, 6).start()
        @pl.when(l == 1)
        def _():
            wait([cp(af, af_st, 7), cp(dg, dg_st, 8)])
        wait(ldF(l))
        ff_fwd(l)
        @pl.when(l == 0)
        def _():
            start(ldF(1))
            start([cp(af, af_st, 7), cp(dg, dg_st, 8)])
        return 0

    ctok.wait()
    lax.fori_loop(0, 2, fwd, 0)
    c_so = cp(xs.at[y + 1], so, 9)
    c_so.start()
    ccot.wait()
    cm.wait_all()

    def up_slot(s):
        return jnp.where(s == 3, 5, s + 1)

    def head_back(s, scale):
        us = up_slot(s)

        def body(i, c):
            a, b = c
            r = pl.ds(pl.multiple_of(i * 64, 64), 64)
            u = xs[us, r, :].astype(F32)
            g = (u * scale).astype(BF16)
            b8 = fold8(u * br[s, r, :].astype(F32))
            br[s, r, :] = g
            return a + b8, b + fold8(g.astype(F32))
        z = jnp.zeros((8, D), F32)
        a, b = lax.fori_loop(0, R // 64, body, (z, z), unroll=UL)
        return rowsum(a), rowsum(b)

    def tail_back(s, gain):
        us = up_slot(s)

        def body(i, c):
            a, b = c
            r = pl.ds(pl.multiple_of(i * 64, 64), 64)
            x = xs[s, r, :].astype(F32)
            gl = T[0, r, :]
            ce = x - jnp.mean(x, -1, keepdims=True)
            rs = lax.rsqrt(jnp.mean(ce * ce, -1, keepdims=True) + EPS)
            n = ce * rs
            gn = gl * n
            t = gl * gain
            u = xs[us, r, :].astype(F32)
            o = u + rs * (t - jnp.mean(t, -1, keepdims=True) - n * jnp.mean(t * n, -1, keepdims=True))
            xs[s, r, :] = o.astype(BF16)
            return a + fold8(gn), b + fold8(gl)
        z = jnp.zeros((8, D), F32)
        a, b = lax.fori_loop(0, R // 64, body, (z, z), unroll=UL)
        @pl.when(y == s)
        def _():
            cp(xs.at[s], go, 10).start()
        return rowsum(a), rowsum(b)

    def put_rows(dst, b, val, nb):
        for o in range(16):
            zz, xx, cc = o // 8, (o // 2) % 4, o % 2
            rows = val[24 * o:24 * o + 24, :]
            chunk = jnp.concatenate([rows[:, 384 * k:384 * (k + 1)] for k in range(nb)], 0)
            dst[cc, 2 * b + zz, xx] = chunk.astype(BF16)

    def ff_bwd(l):
        s = 2 * l + 1
        row = lambda ref: ref[pl.ds(l, 1), :]
        v0 = l * 16
        sg, dbg = head_back(s, row(fsc))
        vsc[pl.ds(v0 + 9, 1), :] = sg
        vsc[pl.ds(v0 + 8, 1), :] = dbg
        @pl.when(l == 0)
        def _():
            cm.s1_start(1, 1)
            cm.y_start(0, 1)
        g = br[s]
        for j in range(4):
            c = slice(D * j, D * (j + 1))
            ga = dot_rt(g, w_dn[c, :])
            gbef = (ga * dg[:, c].astype(F32)).astype(BF16)
            dg[:, c] = gbef
            vsc[pl.ds(v0 + 10 + j, 1), :] = rowsum(fold8(gbef.astype(F32)))
        @pl.when(l == 0)
        def _():
            cm.s2_start(1, 1)
        @pl.when(y < 2)
        def _():
            def b2(b, _):
                a = low[s, :, pl.ds(pl.multiple_of(b * 384, 128), 384)]
                put_rows(fch, b, dot_lt(a, dg[:, pl.ds(pl.multiple_of(y * 1536, 128), 1536)]), 4)
                return 0
            lax.fori_loop(0, 2, b2, 0)
        @pl.when(y >= 2)
        def _():
            gq = br[s, :, pl.ds(pl.multiple_of((y - 2) * 384, 128), 384)]
            def b4(zz, _):
                a = af[:, pl.ds(pl.multiple_of(zz * 768, 128), 768)]
                val = dot_lt(a, gq).astype(BF16)
                for o in range(8):
                    fch[o % 2, zz, o // 2] = val[96 * o:96 * o + 96, :]
                return 0
            lax.fori_loop(0, 4, b4, 0)
        cm.c_start(0, l)
        T[0] = dot_rt(dg[...], w_up[...])
        @pl.when(l == 1)
        def _():
            c_so.wait()
        gg, sh = tail_back(s, row(fg))
        vsc[pl.ds(v0 + 6, 1), :] = gg
        vsc[pl.ds(v0 + 7, 1), :] = sh

    def attn_bwd(l):
        s = 2 * l
        row = lambda ref: ref[pl.ds(l, 1), :]
        v0 = l * 16
        sg, obg = head_back(s, row(asc))
        vsc[pl.ds(v0 + 5, 1), :] = sg
        vsc[pl.ds(v0 + 4, 1), :] = obg
        cm.s1_start(0, l)
        @pl.when(l == 0)
        def _():
            cm.y_start(1, 1)
        low[s + 1] = dot_rt(br[s], w_out[...]).astype(BF16)
        def pair(it, _):
            mb, g = it // 6, it % 6
            rows, cols, q, km, vm = masks(g, mb, l)
            dop = low[s + 1, rows, cols]
            dp = dot_rt(dop, vm)
            e = E[it]
            ef = e.astype(F32)
            pt = ef * dp
            in0 = jnp.sum(pt[:, :MB], -1, keepdims=True) / jnp.sum(ef[:, :MB], -1, keepdims=True)
            in1 = jnp.sum(pt[:, MB:], -1, keepdims=True) / jnp.sum(ef[:, MB:], -1, keepdims=True)
            ds = jnp.concatenate([pt[:, :MB] - ef[:, :MB] * in0, pt[:, MB:] - ef[:, MB:] * in1], 1).astype(BF16)
            dsf = ds.astype(F32)
            @pl.when(mb == 0)
            def _():
                T[head_block(2 * g)] = dsf[:, :MB]
                T[head_block(2 * g + 1)] = dsf[:, MB:]
            @pl.when(mb == 1)
            def _():
                for k in range(2):
                    b = head_block(2 * g + k)
                    T[b] = T[b] + dsf[:, MB * k:MB * k + MB]
            dv = dot_lt(e, dop)
            dk = dot_lt(ds, q)
            dq = dot(ds, km) * 0.125
            hm = lane < 64
            c0 = pl.multiple_of(g * 128, 128)
            qkv[l, rows, pl.ds(c0, 128)] = dq.astype(BF16)
            qkv[l, rows, pl.ds(D + c0, 128)] = jnp.where(hm, dk[:MB], dk[MB:]).astype(BF16)
            qkv[l, rows, pl.ds(2 * D + c0, 128)] = jnp.where(hm, dv[:MB], dv[MB:]).astype(BF16)
            return 0
        with jax.named_scope('pairs'):
            lax.fori_loop(0, 12, pair, 0, unroll=UP)
        cm.s2_start(0, l)
        def fo(h, _):
            a = T[head_block(h)]
            a = jnp.concatenate([a, jnp.zeros((MB, MB), F32)], 1)
            n = MB // 2
            while n >= 1:
                a = a[n:, :] + pltpu.roll(a[:n, :], n, 1)
                n //= 2
            Dsc[pl.ds(h, 1), :] = a
            return 0
        with jax.named_scope('fold'):
            lax.fori_loop(0, H, fo, 0, unroll=UF)
        tg = lax.dot_general(Dsc[...], sel, (((1,), (1,)), ((), ())), precision=lax.Precision.HIGHEST, preferred_element_type=F32)
        vsc[32:48, pl.ds(pl.multiple_of(l * 128, 128), 128)] = jnp.concatenate([tg, jnp.zeros((16, 96), F32)], 1)
        def cs(i, c):
            a, b = c
            r = pl.ds(pl.multiple_of(i * 64, 64), 64)
            return a + fold8(qkv[l, r, 0:D].astype(F32)), b + fold8(qkv[l, r, 2 * D:3 * D].astype(F32))
        z = jnp.zeros((8, D), F32)
        a, b = lax.fori_loop(0, R // 64, cs, (z, z), unroll=UL)
        vsc[pl.ds(v0 + 2, 1), :] = rowsum(a)
        vsc[pl.ds(v0 + 3, 1), :] = rowsum(b)
        @pl.when(y < 3)
        def _():
            def b2(b, _):
                a = low[s, :, pl.ds(pl.multiple_of(b * 384, 128), 384)]
                put_rows(ach, b, dot_lt(a, qkv[l, :, pl.ds(pl.multiple_of(y * D, 128), D)]), 2)
                return 0
            lax.fori_loop(0, 2, b2, 0)
        @pl.when(y == 3)
        def _():
            def b2(b, _):
                a = mixed[l, :, pl.ds(pl.multiple_of(b * 384, 128), 384)]
                put_rows(ach, b, dot_lt(a, br[s]), 2)
                return 0
            lax.fori_loop(0, 2, b2, 0)
        cm.c_start(1, l)
        T[0] = dot_rt(qkv[l], w_in[...])
        @pl.when(l == 0)
        def _():
            cm.s1_start(1, 0)
            cm.y_start(0, 0)
        gg, sh = tail_back(s, row(ag))
        vsc[pl.ds(v0 + 0, 1), :] = gg
        vsc[pl.ds(v0 + 1, 1), :] = sh

    vsc[...] = jnp.zeros_like(vsc)
    Dsc[...] = jnp.zeros_like(Dsc)

    def bwd(i, _):
        l = 1 - i
        @pl.when(l == 0)
        def _():
            wait(ldF(0))
            wait([cp(af_st, af, 7), cp(dg_st, dg, 8)])
        ff_bwd(l)
        @pl.when(l == 1)
        def _():
            start(ldF(0))
            start([cp(af_st, af, 7), cp(dg_st, dg, 8)])
        @pl.when(l == 0)
        def _():
            wait(ldA(0))
            wait([cp(e_st, E, 6)])
        attn_bwd(l)
        @pl.when(l == 1)
        def _():
            start(ldA(0))
            cp(e_st, E, 6).start()
        return 0
    lax.fori_loop(0, 2, bwd, 0)
    cm.v_start(0)
    cm.s2_start(1, 0)
    cm.v_finish(0)
    cm.v_start(1)
    cm.y_start(1, 0)
    cm.v_finish(1)
    cm.v_start(2)
    cp(xs.at[y], go, 10).wait()
    cm.v_finish(2)
    for l in range(2):
        for k in range(2):
            cm.y_done(k, l)


def run_chain(tokens, cotangent, pages, bucket, ag, ash, win, qb, vb, tab, wout, ob, asc, fg, fsh, wup, ub, wdn, db, fsc):
    tok = tokens.reshape(R, D)
    cot = cotangent.reshape(R, D)
    bucket = bucket.reshape(1, 511)
    tab = jnp.transpose(tab, (1, 0, 2))
    ANY = pl.BlockSpec(memory_space=pl.ANY)
    V = pl.BlockSpec(memory_space=pltpu.VMEM)
    sds = jax.ShapeDtypeStruct
    outs = (sds((R, D), BF16), sds((R, D), BF16), sds((4, 288, 384), BF16), sds((48, D), F32),
            sds((12, MB, 512), BF16), sds((R, FF), BF16), sds((R, FF), BF16))
    vm = pltpu.VMEM
    S = pltpu.SemaphoreType.DMA
    scratch = [
        vm((6, R, D), BF16), vm((4, R, D), BF16), vm((2, R, 3 * D), BF16), vm((12, MB, 512), BF16),
        vm((2, R, D), BF16), vm((4, R, D), BF16), vm((R, FF), BF16), vm((R, FF), BF16),
        vm((D, 3 * D), BF16), vm((D, D), BF16), vm((D, FF), BF16), vm((FF, D), BF16),
        vm((2, R, D), F32),
        vm((2, 2, MB, 128), BF16), vm((16, 512), F32), vm((1, 512), jnp.int32), vm((2, 4, 4, 96, 384), BF16), vm((2, 4, 4, 48, 384), BF16),
        vm((4, 4, 144, 384), BF16), vm((3, 4, 288, 384), BF16), vm((3, 288, 384), BF16), vm((4, 288, 384), BF16), vm((7, 48, D), F32),
        S((11,)), S((4, 4, 2, 4)), S((4, 4, 2, 4)), S((7,)), S((7,)), pltpu.SemaphoreType.REGULAR((2,)),
    ]
    return pl.pallas_call(
        chain,
        out_shape=outs,
        in_specs=[ANY, ANY, V, V, V, V, ANY, V, V, V, ANY, V, V, V, V, ANY, V, ANY, V, V],
        out_specs=(ANY, ANY, V, V, ANY, ANY, ANY),
        scratch_shapes=scratch,
        compiler_params=pltpu.CompilerParams(vmem_limit_bytes=63400000, collective_id=0, has_side_effects=True),
        name="chain",
    )(tok, cot, pages, bucket, ag, ash, win, qb, vb, tab, wout, ob, asc, fg, fsh, wup, ub, wdn, db, fsc)


def k3(G, vec, a_gain, a_shift, w_in, qb, vb, tab, w_out, ob, asc, fg, fsh, w_up, ub, w_dn, db, fsc):
    d = lax.axis_index("dp")
    for l in range(2):
        for y in range(4):
            f = G[y, 96 * l:96 * l + 96, :].astype(F32)
            a = G[y, 192 + 48 * l:240 + 48 * l, :].astype(F32)
            if y < 2:
                for k in range(4):
                    w_up[l, :, 1536 * y + 384 * k:1536 * y + 384 * (k + 1)] = f[24 * k:24 * k + 24]
            else:
                w_dn[l, :, 384 * (y - 2):384 * (y - 1)] = f
            for k in range(2):
                if y < 3:
                    w_in[l, :, 768 * y + 384 * k:768 * y + 384 * (k + 1)] = a[24 * k:24 * k + 24]
                else:
                    w_out[l, :, 384 * k:384 * (k + 1)] = a[24 * k:24 * k + 24]
        r = pltpu.roll(vec[16 * l:16 * l + 16, :], lax.rem(D - 24 * d, D), 1)[:, :128]
        for ref, i in ((a_gain, 0), (a_shift, 1), (qb, 2), (vb, 3), (ob, 4), (asc, 5), (fg, 6), (fsh, 7), (db, 8), (fsc, 9)):
            ref[l:l + 1, :] = r[i:i + 1, :24]
        row = vec[pl.ds(16 * l + 10 + d // 8, 1), :]
        ub[l:l + 1, :] = pltpu.roll(jnp.broadcast_to(row, (8, D)), lax.rem(D - 96 * lax.rem(d, 8), D), 1)[0:1, :96]
        tab[:, l, :] = vec[32:32 + H, 128 * l:128 * l + NB]


def run_k3(G, vec):
    V = pl.BlockSpec(memory_space=pltpu.VMEM)
    sds = jax.ShapeDtypeStruct
    w = sds((2, 24), F32)
    outs = (w, w, sds((2, 24, 2304), F32), w, w, sds((H, 2, NB), F32), sds((2, 24, D), F32), w, w, w, w, sds((2, 24, FF), F32), sds((2, 96), F32),
            sds((2, 96, D), F32), w, w)
    return pl.pallas_call(k3, out_shape=outs, in_specs=[V, V], out_specs=(V,) * 16, name="unpack",
                          compiler_params=pltpu.CompilerParams(vmem_limit_bytes=32 << 20))(G, vec)


def body(*args):
    so, go, G, v = run_chain(*args)[:4]
    outs = run_k3(G, v)
    return (so.reshape(1, 2, MB, D), go.reshape(1, 2, MB, D)) + tuple(outs[:5]) + (jnp.transpose(outs[5], (1, 0, 2)),) + tuple(outs[6:])


def solution(mesh):
    data, whole = P("dp", None, None), P()
    w1, w2 = P(None, "dp"), P(None, "dp", None)
    return jax.shard_map(
        body,
        mesh=mesh,
        in_specs=(data, data, P("dp", None)) + (whole,) * 17,
        out_specs=(P("section", "dp", None, None),) * 2 + (w1, w1, w2, w1, w1, P(), w2, w1, w1, w1, w1, w2, w1, w2, w1, w1),
        check_vma=False,
    )
```

```python
import functools
import jax
import jax.numpy as jnp
from jax import lax
from jax.experimental import pallas as pl
from jax.experimental.pallas import tpu as pltpu
from jax.sharding import PartitionSpec as P

D, H, HD, FF, NB, MB = 768, 12, 64, 3072, 32, 256
R = 512
EPS = 1e-5
UP, UL = 12, 8
F32, BF16 = jnp.float32, jnp.bfloat16
C0 = 0.7978845608028654
C1 = 0.044715 * C0


def dot(a, b):
    return jnp.dot(a, b, preferred_element_type=F32)


def dot_rt(a, b):
    return lax.dot_general(a, b, (((1,), (1,)), ((), ())), preferred_element_type=F32)


def dot_lt(a, b):
    return lax.dot_general(a, b, (((0,), (0,)), ((), ())), preferred_element_type=F32)


def fold8(v):
    return jnp.sum(v.reshape(v.shape[0] // 8, 8, v.shape[1]), axis=0)


def rowsum(v):
    return jnp.sum(v, axis=0, keepdims=True)


MESH = pl.DeviceIdType.MESH
KINDS = ((96, 48, 0, 0), (48, 32, 192, 96))


class Comm:
    def __init__(self, vecs, fch, ach, rc, rx1, rx2, G, vxs, sems, semr, vsems, vsemr, credit):
        d = lax.axis_index("dp")
        self.y = lax.axis_index("section")
        self.z, self.x, self.c = d // 8, lax.rem(d // 2, 4), lax.rem(d, 2)
        self.vecs, self.own, self.rc, self.G, self.vxs = vecs, (fch, ach), rc, G, vxs
        self.rx1, self.rx2 = rx1, rx2
        self.sems, self.semr, self.vsems, self.vsemr, self.credit = sems, semr, vsems, vsemr, credit

    def dev(self, axis, o):
        at = {"z": self.z, "x": self.x, "c": self.c, "y": self.y}
        at[axis] = o
        return (at["z"] * 8 + at["x"] * 2 + at["c"], at["y"])

    def others(self, axis):
        me = getattr(self, axis)
        if axis == "c":
            return [(1 - me, 0, 0)]
        return [(lax.rem(me + i, 4), 3 - i, i - 1) for i in (2, 1, 3)]

    def signal_all(self):
        b = pltpu.get_barrier_semaphore()
        for axis in "cxzy":
            for o, _, _ in self.others(axis):
                pl.semaphore_signal(b, inc=1, device_id=self.dev(axis, o), device_id_type=MESH)

    def wait_all(self):
        pl.semaphore_wait(pltpu.get_barrier_semaphore(), 10)

    def copy(self, src, dst, sem, device):
        return pltpu.make_async_remote_copy(src_ref=src, dst_ref=dst, send_sem=self.sems.at[sem], recv_sem=self.semr.at[sem],
                                            device_id=device, device_id_type=MESH)

    def rows(self, kind, l, lo, m):
        n, _, g, _ = KINDS[kind]
        return pl.ds(lo, m), pl.ds(pl.multiple_of(g + n * l + lo, 16), m)

    def half(self, kind, h):
        n, a, _, _ = KINDS[kind]
        return (0, a) if h == 0 else (a, n - a)

    def unit(self, kind, l):
        return 2 * (1 - l) + kind

    def c_copy(self, kind, l):
        n, _, _, r = KINDS[kind]
        o = 1 - self.c
        return self.copy(self.own[kind].at[o], self.rc.at[:, :, r:r + n, :], (self.unit(kind, l), 0, 0), self.dev("c", o))

    def c_start(self, kind, l):
        @pl.when(l == 0)
        def _():
            pl.semaphore_wait(self.credit.at[kind], 1)
        self.c_copy(kind, l).start()

    def at(self, kind, axis, i, j, rows):
        own = self.own[kind]
        return own.at[self.c, j, i, rows, :] if axis == "x" else own.at[self.c, i, j, rows, :]

    def hops(self, kind, l, phase):
        out = []
        u = self.unit(kind, l)
        for h in range(2):
            axis, first = ("xz"[h], None) if phase == 1 else ("zx"[h], "xz"[h])
            me = getattr(self, axis)
            mine, every = self.rows(kind, l, *self.half(kind, h))
            j = pl.ds(0, 4) if phase == 1 else getattr(self, first)
            buf = self.rx1 if phase == 1 else self.rx2
            for o, there, here in self.others(axis):
                cps = []
                for slot in (there, here):
                    dst = buf.at[slot, :, every, :] if phase == 1 else buf.at[slot, every, :]
                    cps.append(self.copy(self.at(kind, axis, o, j, mine), dst, (u, phase, 3 * h + slot), self.dev(axis, o)))
                out.append((h, cps[0], cps[1]))
        return out

    def launch(self, kind, l, phase):
        for _, cp, _ in self.hops(kind, l, phase):
            cp.start()

    def land(self, kind, l, phase):
        hops = self.hops(kind, l, phase)
        for h in range(2):
            for hh, _, cp in hops:
                if hh == h:
                    cp.wait_recv()
            axis = "xz"[h] if phase == 1 else "zx"[h]
            me = getattr(self, axis)
            mine, every = self.rows(kind, l, *self.half(kind, h))

            def total(s, parts):
                v = s[...].astype(F32)
                for p in parts:
                    v = v + p.astype(F32)
                s[...] = v.astype(BF16)
            if phase == 1:
                def add(i, _):
                    total(self.at(kind, axis, me, i, mine), [self.rx1[k, i, every, :] for k in range(3)])
                    return 0
                lax.fori_loop(0, 4, add, 0)
            else:
                total(self.at(kind, axis, me, getattr(self, "xz"[h]), mine), [self.rx2[k, every, :] for k in range(3)])
        for _, cp, _ in hops:
            cp.wait_send()

    def step(self, i, kind, l):
        if i == 1:
            n, _, _, r = KINDS[kind]
            own, c = self.own[kind], self.c
            cc = self.c_copy(kind, l)
            cc.wait_recv()

            def add(i, _):
                z, x = i // 4, lax.rem(i, 4)
                own[c, z, x] = (own[c, z, x].astype(F32) + self.rc[z, x, r:r + n, :].astype(F32)).astype(BF16)
                return 0
            lax.fori_loop(0, 16, add, 0)

            @pl.when(l == 1)
            def _():
                pl.semaphore_signal(self.credit.at[kind], inc=1, device_id=self.dev("c", 1 - c), device_id_type=MESH)
            self.launch(kind, l, 1)
            cc.wait_send()
        elif i == 2:
            self.land(kind, l, 1)
            self.launch(kind, l, 2)
        else:
            self.land(kind, l, 2)
            n = KINDS[kind][0]
            _, every = self.rows(kind, l, 0, n)
            self.G[self.y, every, :] = self.own[kind][self.c, self.z, self.x]
            for o, there, _ in self.others("y"):
                self.y_copy(kind, l, o, self.y, there).start()

    def y_copy(self, kind, l, o, slot, there):
        _, every = self.rows(kind, l, 0, KINDS[kind][0])
        part = self.G.at[slot, every, :]
        return self.copy(part, part, (self.unit(kind, l), 3, there), self.dev("y", o))

    def y_done(self, kind, l):
        for o, there, here in self.others("y"):
            self.y_copy(kind, l, o, o, here).wait_recv()
            self.y_copy(kind, l, o, self.y, there).wait_send()

    def vec(self, b):
        return self.vecs[0].at[self.y] if b == 0 else self.vecs[b]

    def v_copy(self, b, stage, o, there):
        i = (0, 1, 4, 7)[stage] + there
        src = self.vec(b)
        dst = self.vxs[b].at[i]
        return pltpu.make_async_remote_copy(src_ref=src, dst_ref=dst, send_sem=self.vsems.at[b, i], recv_sem=self.vsemr.at[b, i],
                                            device_id=self.dev("cxzy"[stage], o), device_id_type=MESH)

    def v_start(self, b, stage):
        if stage:
            self.v_finish(b, stage - 1)
        for o, there, _ in self.others("cxzy"[stage]):
            self.v_copy(b, stage, o, there).start()

    def v_finish(self, b, stage):
        axis = "cxzy"[stage]
        me = getattr(self, axis)
        vec, vx = self.vec(b), self.vxs[b]
        for o, there, here in self.others(axis):
            self.v_copy(b, stage, o, here).wait_recv()
            self.v_copy(b, stage, o, there).wait_send()
            if b == 0 and stage == 3:
                self.vecs[0][o] = vx[7 + here]
        if b == 0 and stage == 3:
            return
        if stage == 0:
            vec[...] = vec[...] + vx[0]
            return
        own = vec[...]
        terms = []
        for p in range(4):
            slot = lax.rem(p - me + 7, 4)
            terms.append(jnp.where(slot == 3, own, vx[(1, 4, 7)[stage - 1] + jnp.minimum(slot, 2)]))
        vec[...] = (terms[0] + terms[1]) + (terms[2] + terms[3])


def head_block(h):
    k = h % 6
    if isinstance(h, int):
        return h // 6, slice(MB * (k // 3), MB * (k // 3) + MB), slice(MB * (k % 3), MB * (k % 3) + MB)
    return h // 6, pl.ds(pl.multiple_of(MB * (k // 3), MB), MB), pl.ds(pl.multiple_of(MB * (k % 3), MB), MB)


def chain(tok, cot, pages, bucket, ag, ash, win, qb, vb, tab, wout, ob, asc, fg, fsh, wup, ub, wdn, db, fsc,
       so, go, G, v0, v2, v3, e_st, af_st, dg_st,
       xs, low, qkv, E, mixed, br, af, dg, w_in, w_out, w_up, w_dn, T, AB, Dsc, bsc, fch, ach,
       rc, rx1, rx2, vx0, vx2, vx3, sem, sems, semr, vsems, vsemr, credit):
    cm = Comm((v0, v2, v3), fch, ach, rc, rx1, rx2, G, (vx0, vx2, vx3), sems, semr, vsems, vsemr, credit)
    y = cm.y
    def cp(src, dst, i):
        return pltpu.make_async_copy(src, dst, sem.at[i])
    def ldA(l):
        return [cp(win.at[l], w_in, 0), cp(wout.at[l], w_out, 1)]
    def ldF(l):
        return [cp(wup.at[l], w_up, 2), cp(wdn.at[l], w_dn, 3)]
    def start(cs):
        for c in cs: c.start()
    def wait(cs):
        for c in cs: c.wait()
    ctok = cp(tok, xs.at[0], 4)
    ccot = cp(cot, xs.at[5], 5)
    ctok.start()
    start(ldA(0))
    start(ldF(0))
    ccot.start()
    cm.signal_all()
    bsc[...] = jnp.full((1, 512), -1, jnp.int32)
    bsc[:, :511] = bucket[...]
    lane = lax.broadcasted_iota(jnp.int32, (1, 128), 1)
    m0 = (lane < 64).astype(F32).astype(BF16)
    m1 = (lane >= 64).astype(F32).astype(BF16)
    lanef = lax.broadcasted_iota(jnp.int32, (MB, 128), 1).astype(F32)
    for mb in range(2):
        pf = jnp.broadcast_to(pages[mb:mb + 1, :].astype(F32), (128, MB)).T
        same = pf == lanef
        AB[0, mb] = jnp.where(same | (lanef > 7.5), 0.0, -1e30).astype(BF16)
        AB[1, mb] = jnp.where(same, 1.0, 0.0).astype(BF16)
    turn = (lax.broadcasted_iota(jnp.int32, (512, 512), 0) + lax.broadcasted_iota(jnp.int32, (512, 512), 1) == 510).astype(F32).astype(BF16)
    turned = dot(jnp.broadcast_to(bsc[...].astype(F32), (16, 512)).astype(BF16), turn)[0:1, :]
    turned = jnp.where(lax.broadcasted_iota(jnp.int32, (1, 512), 1) == 511, -1.0, turned)
    sel = (lax.broadcasted_iota(jnp.int32, (NB, 512), 0).astype(F32) == turned).astype(F32)

    def layernorm(s, gain, shift):
        def body(i, _):
            r = pl.ds(pl.multiple_of(i * 64, 64), 64)
            x = xs[s, r, :].astype(F32)
            c = x - jnp.mean(x, -1, keepdims=True)
            n = c * lax.rsqrt(jnp.mean(c * c, -1, keepdims=True) + EPS)
            low[s, r, :] = (n * gain + shift).astype(BF16)
            return 0
        lax.fori_loop(0, R // 64, body, 0, unroll=UL)

    def residual(s, val, bias, scale):
        b = val + bias
        br[s] = b.astype(BF16)
        xs[s + 1] = (xs[s].astype(F32) + scale * b).astype(BF16)

    def masks(g, mb, l):
        rows = pl.ds(pl.multiple_of(mb * MB, MB), MB)
        c = pl.multiple_of(g * 128, 128)
        q = qkv[l, rows, pl.ds(c, 128)]
        k = qkv[l, rows, pl.ds(D + c, 128)]
        v = qkv[l, rows, pl.ds(2 * D + c, 128)]
        km = jnp.concatenate([k * m0, k * m1], 0)
        vm = jnp.concatenate([v * m0, v * m1], 0)
        return rows, pl.ds(c, 128), q, km, vm

    def attn_fwd(l):
        s = 2 * l
        row = lambda ref: ref[pl.ds(l, 1), :]
        obias = lax.dot_general(tab[:, pl.ds(l, 1), :].reshape(H, NB), sel, (((1,), (0,)), ((), ())), precision=lax.Precision.HIGHEST, preferred_element_type=F32)
        def toep():
            base = [pltpu.roll(jnp.broadcast_to(obias[h:h + 1, :], (8, 512)), 257, 1, stride=1, stride_axis=0) for h in range(H)]
            base = jnp.concatenate(base, 0)
            for a in range(MB // 8):
                t = pltpu.roll(base, 8 * a, 1) if a else base
                for h in range(H):
                    p, r, c = head_block(h)
                    T[p, r.start + 8 * a:r.start + 8 * a + 8, c] = t[8 * h:8 * h + 8, :MB]
        with jax.named_scope('toep'):
            toep()
        layernorm(s, row(ag), row(ash))
        x = low[s]
        qkv[l, :, 0:D] = ((dot(x, w_in[:, 0:D]) + row(qb)) * 0.125).astype(BF16)
        qkv[l, :, D:2 * D] = dot(x, w_in[:, D:2 * D]).astype(BF16)
        qkv[l, :, 2 * D:3 * D] = (dot(x, w_in[:, 2 * D:3 * D]) + row(vb)).astype(BF16)
        def pair(it, _):
            mb, g = it // 6, it % 6
            rows, cols, q, km, vm = masks(g, mb, l)
            qx = jnp.concatenate([q, AB[0, mb]], 1)
            kx = jnp.concatenate([km, jnp.concatenate([AB[1, mb]] * 2, 0)], 1)
            sc = dot_rt(kx, qx)
            def soft(v):
                e = jnp.exp(v - jnp.max(v, 0, keepdims=True))
                return e * (1.0 / jnp.sum(e, 0, keepdims=True))
            e = jnp.concatenate([soft(sc[:MB] + T[head_block(2 * g)]), soft(sc[MB:] + T[head_block(2 * g + 1)])], 0).astype(BF16)
            E[it] = e
            mixed[l, rows, cols] = dot_lt(vm, e).T.astype(BF16)
            return 0
        with jax.named_scope('pairs'):
            lax.fori_loop(0, 12, pair, 0, unroll=UP)
        residual(s, dot(mixed[l], w_out[...]), row(ob), row(asc))

    def ff_fwd(l):
        s = 2 * l + 1
        row = lambda ref: ref[pl.ds(l, 1), :]
        layernorm(s, row(fg), row(fsh))
        x = low[s]
        for j in range(4):
            u = dot(x, w_up[:, D * j:D * (j + 1)]) + ub[pl.ds(l, 1), D * j:D * (j + 1)]
            u2 = u * u
            t = jnp.tanh(u * (C0 + C1 * u2))
            h = 0.5 * t + 0.5
            af[:, D * j:D * (j + 1)] = (u * h).astype(BF16)
            dg[:, D * j:D * (j + 1)] = (h + (0.5 - 0.5 * t * t) * (u * (C0 + (3 * C1) * u2))).astype(BF16)
        for j in range(2):
            r = slice(256 * j, 256 * j + 256)
            b = dot(af[r], w_dn[...]) + row(db)
            br[s, r] = b.astype(BF16)
            xs[s + 1, r] = (xs[s, r].astype(F32) + row(fsc) * b).astype(BF16)

    def fwd(l, _):
        @pl.when(l == 1)
        def _():
            wait([cp(E, e_st, 6)])
        wait(ldA(l))
        attn_fwd(l)
        @pl.when(l == 0)
        def _():
            start(ldA(1))
            cp(E, e_st, 6).start()
        @pl.when(l == 1)
        def _():
            wait([cp(af, af_st, 7), cp(dg, dg_st, 8)])
        wait(ldF(l))
        ff_fwd(l)
        @pl.when(l == 0)
        def _():
            start(ldF(1))
            start([cp(af, af_st, 7), cp(dg, dg_st, 8)])
        return 0

    ctok.wait()
    lax.fori_loop(0, 2, fwd, 0)
    c_so = cp(xs.at[y + 1], so, 9)
    c_so.start()
    ccot.wait()
    cm.wait_all()

    def up_slot(s):
        return jnp.where(s == 3, 5, s + 1)

    def head_back(s, scale):
        us = up_slot(s)

        def body(i, c):
            a, b = c
            r = pl.ds(pl.multiple_of(i * 64, 64), 64)
            u = xs[us, r, :].astype(F32)
            g = (u * scale).astype(BF16)
            b8 = fold8(u * br[s, r, :].astype(F32))
            br[s, r, :] = g
            return a + b8, b + fold8(g.astype(F32))
        z = jnp.zeros((8, D), F32)
        a, b = lax.fori_loop(0, R // 64, body, (z, z), unroll=UL)
        return rowsum(a), rowsum(b)

    def tail_back(s, gain):
        us = up_slot(s)

        def body(i, c):
            a, b = c
            r = pl.ds(pl.multiple_of(i * 64, 64), 64)
            x = xs[s, r, :].astype(F32)
            gl = T[0, r, :]
            ce = x - jnp.mean(x, -1, keepdims=True)
            rs = lax.rsqrt(jnp.mean(ce * ce, -1, keepdims=True) + EPS)
            n = ce * rs
            gn = gl * n
            t = gl * gain
            u = xs[us, r, :].astype(F32)
            o = u + rs * (t - jnp.mean(t, -1, keepdims=True) - n * jnp.mean(t * n, -1, keepdims=True))
            xs[s, r, :] = o.astype(BF16)
            return a + fold8(gn), b + fold8(gl)
        z = jnp.zeros((8, D), F32)
        a, b = lax.fori_loop(0, R // 64, body, (z, z), unroll=UL)
        @pl.when(y == s)
        def _():
            cp(xs.at[s], go, 10).start()
        return rowsum(a), rowsum(b)

    def put_rows(dst, b, val, nb):
        for o in range(16):
            zz, xx, cc = o // 8, (o // 2) % 4, o % 2
            rows = val[24 * o:24 * o + 24, :]
            chunk = jnp.concatenate([rows[:, 384 * k:384 * (k + 1)] for k in range(nb)], 0)
            dst[cc, 2 * b + zz, xx] = chunk.astype(BF16)

    def ff_bwd(l):
        s = 2 * l + 1
        row = lambda ref: ref[pl.ds(l, 1), :]
        sg, dbg = head_back(s, row(fsc))
        v0[l, 3:4, :] = sg
        v0[l, 2:3, :] = dbg
        g = br[s]
        for j in range(4):
            c = slice(D * j, D * (j + 1))
            ga = dot_rt(g, w_dn[c, :])
            gbef = (ga * dg[:, c].astype(F32)).astype(BF16)
            dg[:, c] = gbef
            v0[l, 4 + j:5 + j, :] = rowsum(fold8(gbef.astype(F32)))
        @pl.when(l == 0)
        def _():
            cm.step(3, 0, 1)
        @pl.when(y < 2)
        def _():
            def b2(b, _):
                a = low[s, :, pl.ds(pl.multiple_of(b * 384, 128), 384)]
                put_rows(fch, b, dot_lt(a, dg[:, pl.ds(pl.multiple_of(y * 1536, 128), 1536)]), 4)
                return 0
            lax.fori_loop(0, 2, b2, 0)
        @pl.when(y >= 2)
        def _():
            gq = br[s, :, pl.ds(pl.multiple_of((y - 2) * 384, 128), 384)]
            def b4(zz, _):
                a = af[:, pl.ds(pl.multiple_of(zz * 768, 128), 768)]
                val = dot_lt(a, gq).astype(BF16)
                for o in range(8):
                    fch[o % 2, zz, o // 2] = val[96 * o:96 * o + 96, :]
                return 0
            lax.fori_loop(0, 4, b4, 0)
        cm.c_start(0, l)
        for j in range(2):
            T[0, 256 * j:256 * j + 256] = dot_rt(dg[256 * j:256 * j + 256], w_up[...])
        @pl.when(l == 0)
        def _():
            cm.step(2, 1, 1)
        @pl.when(l == 1)
        def _():
            c_so.wait()
        gg, sh = tail_back(s, row(fg))
        v0[l, 0:1, :] = gg
        v0[l, 1:2, :] = sh

    def attn_bwd(l):
        s = 2 * l
        row = lambda ref: ref[pl.ds(l, 1), :]
        sg, obg = head_back(s, row(asc))

        def small(i, val):
            @pl.when(l == 1)
            def _():
                v0[2, i:i + 1, :] = val
            @pl.when(l == 0)
            def _():
                if i < 2:
                    v2[i:i + 1, :] = val
                else:
                    v0[3, i:i + 1, :] = val
        small(5, sg)
        small(4, obg)
        cm.step(1, 0, l)
        low[s + 1] = dot_rt(br[s], w_out[...]).astype(BF16)
        T[...] = jnp.zeros_like(T)

        def pair(mb, g):
            it = 6 * mb + g
            rows, cols, q, km, vm = masks(g, mb, l)
            dop = low[s + 1, rows, cols]
            dp = dot_rt(vm, dop)
            e = E[it]
            ef = e.astype(F32)
            pt = ef * dp
            in0 = jnp.sum(pt[:MB], 0, keepdims=True) / jnp.sum(ef[:MB], 0, keepdims=True)
            in1 = jnp.sum(pt[MB:], 0, keepdims=True) / jnp.sum(ef[MB:], 0, keepdims=True)
            ds = jnp.concatenate([pt[:MB] - ef[:MB] * in0, pt[MB:] - ef[MB:] * in1], 0).astype(BF16)
            for k in range(2):
                b = head_block(2 * g + k)
                T[b] = T[b] + ds[MB * k:MB * k + MB].astype(F32)
            dv = dot(e, dop)
            dk = dot(ds, q)
            dq = (dot_lt(km, ds) * 0.125).T
            hm = lane < 64
            c0 = pl.multiple_of(g * 128, 128)
            qkv[l, rows, pl.ds(c0, 128)] = dq.astype(BF16)
            qkv[l, rows, pl.ds(D + c0, 128)] = jnp.where(hm, dk[:MB], dk[MB:]).astype(BF16)
            qkv[l, rows, pl.ds(2 * D + c0, 128)] = jnp.where(hm, dv[:MB], dv[MB:]).astype(BF16)

        def half(mb, _):
            for g in range(6):
                pair(mb, g)
            @pl.when((mb == 0) & (l == 0))
            def _():
                cm.step(3, 1, 1)
            return 0
        lax.fori_loop(0, 2, half, 0)
        def cs(i, c):
            a, b = c
            r = pl.ds(pl.multiple_of(i * 64, 64), 64)
            return a + fold8(qkv[l, r, 0:D].astype(F32)), b + fold8(qkv[l, r, 2 * D:3 * D].astype(F32))
        z = jnp.zeros((8, D), F32)
        a, b = lax.fori_loop(0, R // 64, cs, (z, z), unroll=UL)
        small(2, rowsum(a))
        small(3, rowsum(b))
        @pl.when(l == 0)
        def _():
            cm.v_start(0, 0)
        @pl.when(y < 3)
        def _():
            def b2(b, _):
                a = low[s, :, pl.ds(pl.multiple_of(b * 384, 128), 384)]
                put_rows(ach, b, dot_lt(a, qkv[l, :, pl.ds(pl.multiple_of(y * D, 128), D)]), 2)
                return 0
            lax.fori_loop(0, 2, b2, 0)
        @pl.when(y == 3)
        def _():
            def b2(b, _):
                a = mixed[l, :, pl.ds(pl.multiple_of(b * 384, 128), 384)]
                put_rows(ach, b, dot_lt(a, br[s]), 2)
                return 0
            lax.fori_loop(0, 2, b2, 0)
        cm.c_start(1, l)
        def fo(h, _):
            h = 3 * y + h
            a = T[head_block(h)]
            a = jnp.concatenate([a, jnp.zeros((MB, MB), F32)], 1)
            n = MB // 2
            while n >= 1:
                a = a[n:, :] + pltpu.roll(a[:n, :], n, 1)
                n //= 2
            Dsc[pl.ds(h, 1), :] = a
            return 0
        with jax.named_scope('fold'):
            lax.fori_loop(0, 3, fo, 0, unroll=True)
        tg = lax.dot_general(Dsc[...], sel, (((1,), (1,)), ((), ())), precision=lax.Precision.HIGHEST, preferred_element_type=F32)
        v3[pl.ds(pl.multiple_of(l * 16, 16), 16), :] = jnp.concatenate([tg, jnp.zeros((16, 96), F32)], 1)
        @pl.when(l == 0)
        def _():
            cm.v_start(2, 0)
            cm.v_start(0, 1)
        T[0] = dot_rt(qkv[l], w_in[...])
        cm.step(1, 1, l)
        @pl.when(l == 0)
        def _():
            cm.v_start(2, 1)
        cm.step(2, 0, l)
        gg, sh = tail_back(s, row(ag))
        small(0, gg)
        small(1, sh)

    v0[...] = jnp.zeros_like(v0)
    Dsc[...] = jnp.zeros_like(Dsc)

    def bwd(i, _):
        l = 1 - i
        @pl.when(l == 0)
        def _():
            wait(ldF(0))
            wait([cp(af_st, af, 7), cp(dg_st, dg, 8)])
        ff_bwd(l)
        @pl.when(l == 1)
        def _():
            start(ldF(0))
            start([cp(af_st, af, 7), cp(dg_st, dg, 8)])
        @pl.when(l == 0)
        def _():
            wait(ldA(0))
            wait([cp(e_st, E, 6)])
        attn_bwd(l)
        @pl.when(l == 1)
        def _():
            start(ldA(0))
            cp(e_st, E, 6).start()
        return 0
    lax.fori_loop(0, 2, bwd, 0)
    cm.v_start(1, 0)
    cm.v_start(0, 2)
    cm.v_start(2, 2)
    cm.v_start(1, 1)
    cm.step(2, 1, 0)
    cm.step(3, 0, 0)
    cm.v_start(0, 3)
    cm.v_start(2, 3)
    cm.v_start(1, 2)
    cm.step(3, 1, 0)
    cm.v_finish(0, 3)
    cm.v_finish(2, 3)
    cm.v_finish(1, 2)
    cp(xs.at[y], go, 10).wait()
    for l in (1, 0):
        for k in range(2):
            cm.y_done(k, l)


def run_chain(tokens, cotangent, pages, bucket, ag, ash, win, qb, vb, tab, wout, ob, asc, fg, fsh, wup, ub, wdn, db, fsc):
    tok = tokens.reshape(R, D)
    cot = cotangent.reshape(R, D)
    bucket = bucket.reshape(1, 511)
    tab = jnp.transpose(tab, (1, 0, 2))
    ANY = pl.BlockSpec(memory_space=pl.ANY)
    V = pl.BlockSpec(memory_space=pltpu.VMEM)
    sds = jax.ShapeDtypeStruct
    outs = (sds((R, D), BF16), sds((R, D), BF16), sds((4, 288, 384), BF16), sds((4, 8, D), F32), sds((2, D), F32), sds((32, 128), F32),
            sds((12, 512, MB), BF16), sds((R, FF), BF16), sds((R, FF), BF16))
    vm = pltpu.VMEM
    S = pltpu.SemaphoreType.DMA
    scratch = [
        vm((6, R, D), BF16), vm((4, R, D), BF16), vm((2, R, 3 * D), BF16), vm((12, 512, MB), BF16),
        vm((2, R, D), BF16), vm((4, R, D), BF16), vm((R, FF), BF16), vm((R, FF), BF16),
        vm((D, 3 * D), BF16), vm((D, D), BF16), vm((D, FF), BF16), vm((FF, D), BF16),
        vm((2, R, D), F32),
        vm((2, 2, MB, 128), BF16), vm((16, 512), F32), vm((1, 512), jnp.int32), vm((2, 4, 4, 96, 384), BF16), vm((2, 4, 4, 48, 384), BF16),
        vm((4, 4, 144, 384), BF16), vm((3, 4, 288, 384), BF16), vm((3, 288, 384), BF16),
        vm((10, 8, D), F32), vm((7, 2, D), F32), vm((10, 32, 128), F32),
        S((11,)), S((4, 4, 6)), S((4, 4, 6)), S((3, 10)), S((3, 10)), pltpu.SemaphoreType.REGULAR((2,)),
    ]
    return pl.pallas_call(
        chain,
        out_shape=outs,
        in_specs=[ANY, ANY, V, V, V, V, ANY, V, V, V, ANY, V, V, V, V, ANY, V, ANY, V, V],
        out_specs=(ANY, ANY, V, V, V, V, ANY, ANY, ANY),
        scratch_shapes=scratch,
        compiler_params=pltpu.CompilerParams(vmem_limit_bytes=63400000, collective_id=0, has_side_effects=True),
        name="chain",
    )(tok, cot, pages, bucket, ag, ash, win, qb, vb, tab, wout, ob, asc, fg, fsh, wup, ub, wdn, db, fsc)


def unpack(so_in, go_in, G_in, v0_in, v2_in, v3_in, so, go, a_gain, a_shift, w_in, qb, vb, tab, w_out, ob, asc, fg, fsh, w_up, ub, w_dn, db, fsc, G, v0, v2, v3, so_mid, go_mid, sem):
    d = lax.axis_index("dp")
    pairs = ((G_in, G), (v0_in, v0), (v2_in, v2), (v3_in, v3), (so_in, so_mid), (go_in, go_mid))
    copies = [pltpu.make_async_copy(a, b, sem.at[i]) for i, (a, b) in enumerate(pairs)]
    for cp in copies:
        cp.start()
    for cp in copies[:4]:
        cp.wait()
    last = [pltpu.make_async_copy(a, b, sem.at[6 + i]) for i, (a, b) in enumerate(((so_mid, so), (go_mid, go)))]
    for a, b in zip(copies[4:], last):
        a.wait()
        b.start()
    for l in range(2):
        for y in range(4):
            f = G[y, 96 * l:96 * l + 96, :].astype(F32)
            a = G[y, 192 + 48 * l:240 + 48 * l, :].astype(F32)
            if y < 2:
                for k in range(4):
                    w_up[l, :, 1536 * y + 384 * k:1536 * y + 384 * (k + 1)] = f[24 * k:24 * k + 24]
            else:
                w_dn[l, :, 384 * (y - 2):384 * (y - 1)] = f
            for k in range(2):
                if y < 3:
                    w_in[l, :, 768 * y + 384 * k:768 * y + 384 * (k + 1)] = a[24 * k:24 * k + 24]
                else:
                    w_out[l, :, 384 * k:384 * (k + 1)] = a[24 * k:24 * k + 24]
    shift = lax.rem(D - 24 * d, D)
    r0 = [pltpu.roll(v0[i], shift, 1)[:, :128] for i in range(4)]
    r2 = pltpu.roll(jnp.concatenate([v2[...], jnp.zeros((6, D), F32)], 0), shift, 1)[:, :128]
    for i, ref in enumerate((fg, fsh, db, fsc)):
        for l in range(2):
            ref[l:l + 1, :] = r0[l][i:i + 1, :24]
    for i, ref in enumerate((a_gain, a_shift, qb, vb, ob, asc)):
        ref[1:2, :] = r0[2][i:i + 1, :24]
        ref[0:1, :] = (r2 if i < 2 else r0[3])[i:i + 1, :24]
    for l in range(2):
        row = v0[l, pl.ds(4 + d // 8, 1), :]
        ub[l:l + 1, :] = pltpu.roll(jnp.broadcast_to(row, (8, D)), lax.rem(D - 96 * lax.rem(d, 8), D), 1)[0:1, :96]
        tab[:, l, :] = v3[16 * l:16 * l + H, :NB]
    for cp in last:
        cp.wait()


def run_unpack(*args):
    V = pl.BlockSpec(memory_space=pltpu.VMEM)
    ANY = pl.BlockSpec(memory_space=pl.ANY)
    sds = jax.ShapeDtypeStruct
    w = sds((2, 24), F32)
    outs = (sds((R, D), BF16), sds((R, D), BF16), w, w, sds((2, 24, 2304), F32), w, w, sds((H, 2, NB), F32), sds((2, 24, D), F32), w, w, w, w,
            sds((2, 24, FF), F32), sds((2, 96), F32), sds((2, 96, D), F32), w, w)
    vm = pltpu.VMEM
    return pl.pallas_call(
        unpack, out_shape=outs, in_specs=[ANY] * 6, out_specs=(ANY, ANY) + (V,) * 16, name="unpack",
        scratch_shapes=[vm((4, 288, 384), BF16), vm((4, 8, D), F32), vm((2, D), F32), vm((32, 128), F32), vm((R, D), BF16), vm((R, D), BF16), pltpu.SemaphoreType.DMA((8,))],
        compiler_params=pltpu.CompilerParams(vmem_limit_bytes=63400000))(*args)


def body(*args):
    so, go, *outs = run_unpack(*run_chain(*args)[:6])
    outs[5] = jnp.transpose(outs[5], (1, 0, 2))
    return (so.reshape(1, 2, MB, D), go.reshape(1, 2, MB, D)) + tuple(outs)


def solution(mesh):
    data, whole = P("dp", None, None), P()
    w1, w2 = P(None, "dp"), P(None, "dp", None)
    return jax.shard_map(
        body,
        mesh=mesh,
        in_specs=(data, data, P("dp", None)) + (whole,) * 17,
        out_specs=(P("section", "dp", None, None),) * 2 + (w1, w1, w2, w1, w1, P(), w2, w1, w1, w1, w1, w2, w1, w2, w1, w1),
        check_vma=False,
    )
```

```python
import functools
import jax
import jax.numpy as jnp
from jax import lax
from jax.experimental import pallas as pl
from jax.experimental.pallas import tpu as pltpu
from jax.sharding import PartitionSpec as P

D, H, HD, FF, NB, MB = 768, 12, 64, 3072, 32, 256
R = 512
EPS = 1e-5
UP, UL = 12, 8
F32, BF16 = jnp.float32, jnp.bfloat16
C0 = 0.7978845608028654
C1 = 0.044715 * C0


def dot(a, b):
    return jnp.dot(a, b, preferred_element_type=F32)


def dot_rt(a, b):
    return lax.dot_general(a, b, (((1,), (1,)), ((), ())), preferred_element_type=F32)


def dot_lt(a, b):
    return lax.dot_general(a, b, (((0,), (0,)), ((), ())), preferred_element_type=F32)


def fold8(v):
    return jnp.sum(v.reshape(v.shape[0] // 8, 8, v.shape[1]), axis=0)


def rowsum(v):
    return jnp.sum(v, axis=0, keepdims=True)


MESH = pl.DeviceIdType.MESH
KINDS = ((96, 48, 0, 0), (48, 32, 192, 96))


class Comm:
    def __init__(self, vecs, fch, ach, rc, rx1, rx2, G, vxs, sems, semr, vsems, vsemr, credit):
        d = lax.axis_index("dp")
        self.y = lax.axis_index("section")
        self.z, self.x, self.c = d // 8, lax.rem(d // 2, 4), lax.rem(d, 2)
        self.vecs, self.own, self.rc, self.G, self.vxs = vecs, (fch, ach), rc, G, vxs
        self.rx1, self.rx2 = rx1, rx2
        self.sems, self.semr, self.vsems, self.vsemr, self.credit = sems, semr, vsems, vsemr, credit

    def dev(self, axis, o):
        at = {"z": self.z, "x": self.x, "c": self.c, "y": self.y}
        at[axis] = o
        return (at["z"] * 8 + at["x"] * 2 + at["c"], at["y"])

    def others(self, axis):
        me = getattr(self, axis)
        if axis == "c":
            return [(1 - me, 0, 0)]
        return [(lax.rem(me + i, 4), 3 - i, i - 1) for i in (2, 1, 3)]

    def signal_all(self):
        b = pltpu.get_barrier_semaphore()
        for axis in "cxzy":
            for o, _, _ in self.others(axis):
                pl.semaphore_signal(b, inc=1, device_id=self.dev(axis, o), device_id_type=MESH)

    def wait_all(self):
        pl.semaphore_wait(pltpu.get_barrier_semaphore(), 10)

    def copy(self, src, dst, sem, device):
        return pltpu.make_async_remote_copy(src_ref=src, dst_ref=dst, send_sem=self.sems.at[sem], recv_sem=self.semr.at[sem],
                                            device_id=device, device_id_type=MESH)

    def rows(self, kind, l, lo, m):
        n, _, g, _ = KINDS[kind]
        return pl.ds(lo, m), pl.ds(pl.multiple_of(g + n * l + lo, 16), m)

    def half(self, kind, h):
        n, a, _, _ = KINDS[kind]
        return (0, a) if h == 0 else (a, n - a)

    def unit(self, kind, l):
        return 2 * (1 - l) + kind

    def c_copy(self, kind, l):
        n, _, _, r = KINDS[kind]
        o = 1 - self.c
        return self.copy(self.own[kind].at[o], self.rc.at[:, :, r:r + n, :], (self.unit(kind, l), 0, 0), self.dev("c", o))

    def c_start(self, kind, l):
        @pl.when(l == 0)
        def _():
            pl.semaphore_wait(self.credit.at[kind], 1)
        self.c_copy(kind, l).start()

    def at(self, kind, axis, i, j, rows):
        own = self.own[kind]
        return own.at[self.c, j, i, rows, :] if axis == "x" else own.at[self.c, i, j, rows, :]

    def hops(self, kind, l, phase):
        out = []
        u = self.unit(kind, l)
        for h in range(2):
            axis, first = ("xz"[h], None) if phase == 1 else ("zx"[h], "xz"[h])
            me = getattr(self, axis)
            mine, every = self.rows(kind, l, *self.half(kind, h))
            j = pl.ds(0, 4) if phase == 1 else getattr(self, first)
            buf = self.rx1 if phase == 1 else self.rx2
            for o, there, here in self.others(axis):
                cps = []
                for slot in (there, here):
                    dst = buf.at[slot, :, every, :] if phase == 1 else buf.at[slot, every, :]
                    cps.append(self.copy(self.at(kind, axis, o, j, mine), dst, (u, phase, 3 * h + slot), self.dev(axis, o)))
                out.append((h, cps[0], cps[1]))
        return out

    def launch(self, kind, l, phase):
        for _, cp, _ in self.hops(kind, l, phase):
            cp.start()

    def land(self, kind, l, phase):
        hops = self.hops(kind, l, phase)
        for h in range(2):
            for hh, _, cp in hops:
                if hh == h:
                    cp.wait_recv()
            axis = "xz"[h] if phase == 1 else "zx"[h]
            me = getattr(self, axis)
            mine, every = self.rows(kind, l, *self.half(kind, h))

            def total(s, parts):
                v = s[...].astype(F32)
                for p in parts:
                    v = v + p.astype(F32)
                s[...] = v.astype(BF16)
            if phase == 1:
                def add(i, _):
                    total(self.at(kind, axis, me, i, mine), [self.rx1[k, i, every, :] for k in range(3)])
                    return 0
                lax.fori_loop(0, 4, add, 0)
            else:
                total(self.at(kind, axis, me, getattr(self, "xz"[h]), mine), [self.rx2[k, every, :] for k in range(3)])
        for _, cp, _ in hops:
            cp.wait_send()

    def step(self, i, kind, l):
        if i == 1:
            n, _, _, r = KINDS[kind]
            own, c = self.own[kind], self.c
            cc = self.c_copy(kind, l)
            cc.wait_recv()

            def add(i, _):
                z, x = i // 4, lax.rem(i, 4)
                own[c, z, x] = (own[c, z, x].astype(F32) + self.rc[z, x, r:r + n, :].astype(F32)).astype(BF16)
                return 0
            lax.fori_loop(0, 16, add, 0)

            @pl.when(l == 1)
            def _():
                pl.semaphore_signal(self.credit.at[kind], inc=1, device_id=self.dev("c", 1 - c), device_id_type=MESH)
            self.launch(kind, l, 1)
            cc.wait_send()
        elif i == 2:
            self.land(kind, l, 1)
            self.launch(kind, l, 2)
        else:
            self.land(kind, l, 2)
            n = KINDS[kind][0]
            _, every = self.rows(kind, l, 0, n)
            self.G[self.y, every, :] = self.own[kind][self.c, self.z, self.x]
            for o, there, _ in self.others("y"):
                self.y_copy(kind, l, o, self.y, there).start()

    def y_copy(self, kind, l, o, slot, there):
        _, every = self.rows(kind, l, 0, KINDS[kind][0])
        part = self.G.at[slot, every, :]
        return self.copy(part, part, (self.unit(kind, l), 3, there), self.dev("y", o))

    def y_done(self, kind, l):
        for o, there, here in self.others("y"):
            self.y_copy(kind, l, o, o, here).wait_recv()
            self.y_copy(kind, l, o, self.y, there).wait_send()

    def vec(self, b):
        return self.vecs[0].at[self.y] if b == 0 else self.vecs[b]

    def v_copy(self, b, stage, o, there):
        i = (0, 1, 4, 7)[stage] + there
        src = self.vec(b)
        dst = self.vxs[b].at[i]
        return pltpu.make_async_remote_copy(src_ref=src, dst_ref=dst, send_sem=self.vsems.at[b, i], recv_sem=self.vsemr.at[b, i],
                                            device_id=self.dev("cxzy"[stage], o), device_id_type=MESH)

    def v_start(self, b, stage):
        if stage:
            self.v_finish(b, stage - 1)
        for o, there, _ in self.others("cxzy"[stage]):
            self.v_copy(b, stage, o, there).start()

    def v_finish(self, b, stage):
        axis = "cxzy"[stage]
        me = getattr(self, axis)
        vec, vx = self.vec(b), self.vxs[b]
        for o, there, here in self.others(axis):
            self.v_copy(b, stage, o, here).wait_recv()
            self.v_copy(b, stage, o, there).wait_send()
            if b == 0 and stage == 3:
                self.vecs[0][o] = vx[7 + here]
        if b == 0 and stage == 3:
            return
        if stage == 0:
            vec[...] = vec[...] + vx[0]
            return
        own = vec[...]
        terms = []
        for p in range(4):
            slot = lax.rem(p - me + 7, 4)
            terms.append(jnp.where(slot == 3, own, vx[(1, 4, 7)[stage - 1] + jnp.minimum(slot, 2)]))
        vec[...] = (terms[0] + terms[1]) + (terms[2] + terms[3])


def head_block(h):
    k = h % 6
    if isinstance(h, int):
        return h // 6, slice(MB * (k // 3), MB * (k // 3) + MB), slice(MB * (k % 3), MB * (k % 3) + MB)
    return h // 6, pl.ds(pl.multiple_of(MB * (k // 3), MB), MB), pl.ds(pl.multiple_of(MB * (k % 3), MB), MB)


def chain(tok, cot, pages, bucket, ag, ash, win, qb, vb, tab, wout, ob, asc, fg, fsh, wup, ub, wdn, db, fsc,
       so, go, G, v0, v2, v3, e_st, af_st, dg_st,
       xs, low, qkv, E, mixed, br, af, dg, w_in, w_out, w_up, w_dn, T, AB, Dsc, bsc, fch, ach,
       rc, rx1, rx2, vx0, vx2, vx3, sem, sems, semr, vsems, vsemr, credit):
    cm = Comm((v0, v2, v3), fch, ach, rc, rx1, rx2, G, (vx0, vx2, vx3), sems, semr, vsems, vsemr, credit)
    y = cm.y
    def cp(src, dst, i):
        return pltpu.make_async_copy(src, dst, sem.at[i])
    def ldA(l):
        return [cp(win.at[l], w_in, 0), cp(wout.at[l], w_out, 1)]
    def ldF(l):
        return [cp(wup.at[l], w_up, 2), cp(wdn.at[l], w_dn, 3)]
    def start(cs):
        for c in cs: c.start()
    def wait(cs):
        for c in cs: c.wait()
    ctok = cp(tok, xs.at[0], 4)
    ccot = cp(cot, xs.at[5], 5)
    ctok.start()
    start(ldA(0))
    start(ldF(0))
    ccot.start()
    cm.signal_all()
    bsc[...] = jnp.full((1, 512), -1, jnp.int32)
    bsc[:, :511] = bucket[...]
    lane = lax.broadcasted_iota(jnp.int32, (1, 128), 1)
    m0 = (lane < 64).astype(F32).astype(BF16)
    m1 = (lane >= 64).astype(F32).astype(BF16)
    lanef = lax.broadcasted_iota(jnp.int32, (MB, 128), 1).astype(F32)
    for mb in range(2):
        pf = jnp.broadcast_to(pages[mb:mb + 1, :].astype(F32), (128, MB)).T
        same = pf == lanef
        AB[0, mb] = jnp.where(same | (lanef > 7.5), 0.0, -1e30).astype(BF16)
        AB[1, mb] = jnp.where(same, 1.0, 0.0).astype(BF16)
    turn = (lax.broadcasted_iota(jnp.int32, (512, 512), 0) + lax.broadcasted_iota(jnp.int32, (512, 512), 1) == 510).astype(F32).astype(BF16)
    turned = dot(jnp.broadcast_to(bsc[...].astype(F32), (16, 512)).astype(BF16), turn)[0:1, :]
    turned = jnp.where(lax.broadcasted_iota(jnp.int32, (1, 512), 1) == 511, -1.0, turned)
    sel = (lax.broadcasted_iota(jnp.int32, (NB, 512), 0).astype(F32) == turned).astype(F32)

    def layernorm(s, gain, shift):
        def body(i, _):
            r = pl.ds(pl.multiple_of(i * 64, 64), 64)
            x = xs[s, r, :].astype(F32)
            c = x - jnp.mean(x, -1, keepdims=True)
            n = c * lax.rsqrt(jnp.mean(c * c, -1, keepdims=True) + EPS)
            low[s, r, :] = (n * gain + shift).astype(BF16)
            return 0
        lax.fori_loop(0, R // 64, body, 0, unroll=UL)

    def residual(s, val, bias, scale):
        b = val + bias
        br[s] = b.astype(BF16)
        xs[s + 1] = (xs[s].astype(F32) + scale * b).astype(BF16)

    def masks(g, mb, l):
        rows = pl.ds(pl.multiple_of(mb * MB, MB), MB)
        c = pl.multiple_of(g * 128, 128)
        q = qkv[l, rows, pl.ds(c, 128)]
        k = qkv[l, rows, pl.ds(D + c, 128)]
        v = qkv[l, rows, pl.ds(2 * D + c, 128)]
        km = jnp.concatenate([k * m0, k * m1], 0)
        vm = jnp.concatenate([v * m0, v * m1], 0)
        return rows, pl.ds(c, 128), q, km, vm

    def attn_fwd(l):
        s = 2 * l
        row = lambda ref: ref[pl.ds(l, 1), :]
        obias = lax.dot_general(tab[:, pl.ds(l, 1), :].reshape(H, NB), sel, (((1,), (0,)), ((), ())), precision=lax.Precision.HIGHEST, preferred_element_type=F32)
        def toep():
            base = [pltpu.roll(jnp.broadcast_to(obias[h:h + 1, :], (8, 512)), 257, 1, stride=1, stride_axis=0) for h in range(H)]
            base = jnp.concatenate(base, 0)
            for a in range(MB // 8):
                t = pltpu.roll(base, 8 * a, 1) if a else base
                for h in range(H):
                    p, r, c = head_block(h)
                    T[p, r.start + 8 * a:r.start + 8 * a + 8, c] = t[8 * h:8 * h + 8, :MB]
        with jax.named_scope('toep'):
            toep()
        layernorm(s, row(ag), row(ash))
        x = low[s]
        qkv[l, :, 0:D] = ((dot(x, w_in[:, 0:D]) + row(qb)) * 0.125).astype(BF16)
        qkv[l, :, D:2 * D] = dot(x, w_in[:, D:2 * D]).astype(BF16)
        qkv[l, :, 2 * D:3 * D] = (dot(x, w_in[:, 2 * D:3 * D]) + row(vb)).astype(BF16)
        def pair(it, _):
            mb, g = it // 6, it % 6
            rows, cols, q, km, vm = masks(g, mb, l)
            qx = jnp.concatenate([q, AB[0, mb]], 1)
            kx = jnp.concatenate([km, jnp.concatenate([AB[1, mb]] * 2, 0)], 1)
            sc = dot_rt(kx, qx)
            def soft(v):
                e = jnp.exp(v - jnp.max(v, 0, keepdims=True))
                return e * (1.0 / jnp.sum(e, 0, keepdims=True))
            e = jnp.concatenate([soft(sc[:MB] + T[head_block(2 * g)]), soft(sc[MB:] + T[head_block(2 * g + 1)])], 0).astype(BF16)
            E[it] = e
            mixed[l, rows, cols] = dot_lt(vm, e).T.astype(BF16)
            return 0
        with jax.named_scope('pairs'):
            lax.fori_loop(0, 12, pair, 0, unroll=UP)
        residual(s, dot(mixed[l], w_out[...]), row(ob), row(asc))

    def ff_fwd(l):
        s = 2 * l + 1
        row = lambda ref: ref[pl.ds(l, 1), :]
        layernorm(s, row(fg), row(fsh))
        x = low[s]
        for j in range(4):
            u = dot(x, w_up[:, D * j:D * (j + 1)]) + ub[pl.ds(l, 1), D * j:D * (j + 1)]
            u2 = u * u
            t = jnp.tanh(u * (C0 + C1 * u2))
            h = 0.5 * t + 0.5
            af[:, D * j:D * (j + 1)] = (u * h).astype(BF16)
            dg[:, D * j:D * (j + 1)] = (h + (0.5 - 0.5 * t * t) * (u * (C0 + (3 * C1) * u2))).astype(BF16)
        for j in range(2):
            r = slice(256 * j, 256 * j + 256)
            b = dot(af[r], w_dn[...]) + row(db)
            br[s, r] = b.astype(BF16)
            xs[s + 1, r] = (xs[s, r].astype(F32) + row(fsc) * b).astype(BF16)

    def fwd(l, _):
        @pl.when(l == 1)
        def _():
            wait([cp(E, e_st, 6)])
        wait(ldA(l))
        attn_fwd(l)
        @pl.when(l == 0)
        def _():
            start(ldA(1))
            cp(E, e_st, 6).start()
        @pl.when(l == 1)
        def _():
            wait([cp(af, af_st, 7), cp(dg, dg_st, 8)])
        wait(ldF(l))
        ff_fwd(l)
        @pl.when(l == 0)
        def _():
            start(ldF(1))
            start([cp(af, af_st, 7), cp(dg, dg_st, 8)])
        return 0

    ctok.wait()
    lax.fori_loop(0, 2, fwd, 0)
    c_so = cp(xs.at[y + 1], so, 9)
    c_so.start()
    ccot.wait()
    cm.wait_all()

    def up_slot(s):
        return jnp.where(s == 3, 5, s + 1)

    def head_back(s, scale):
        us = up_slot(s)

        def body(i, c):
            a, b = c
            r = pl.ds(pl.multiple_of(i * 64, 64), 64)
            u = xs[us, r, :].astype(F32)
            g = (u * scale).astype(BF16)
            b8 = fold8(u * br[s, r, :].astype(F32))
            br[s, r, :] = g
            return a + b8, b + fold8(g.astype(F32))
        z = jnp.zeros((8, D), F32)
        a, b = lax.fori_loop(0, R // 64, body, (z, z), unroll=UL)
        return rowsum(a), rowsum(b)

    def tail_back(s, gain):
        us = up_slot(s)

        def body(i, c):
            a, b = c
            r = pl.ds(pl.multiple_of(i * 64, 64), 64)
            x = xs[s, r, :].astype(F32)
            gl = T[0, r, :]
            ce = x - jnp.mean(x, -1, keepdims=True)
            rs = lax.rsqrt(jnp.mean(ce * ce, -1, keepdims=True) + EPS)
            n = ce * rs
            gn = gl * n
            t = gl * gain
            u = xs[us, r, :].astype(F32)
            o = u + rs * (t - jnp.mean(t, -1, keepdims=True) - n * jnp.mean(t * n, -1, keepdims=True))
            xs[s, r, :] = o.astype(BF16)
            return a + fold8(gn), b + fold8(gl)
        z = jnp.zeros((8, D), F32)
        a, b = lax.fori_loop(0, R // 64, body, (z, z), unroll=UL)
        @pl.when(y == s)
        def _():
            cp(xs.at[s], go, 10).start()
        return rowsum(a), rowsum(b)

    def put_rows(dst, b, val, nb):
        for o in range(16):
            zz, xx, cc = o // 8, (o // 2) % 4, o % 2
            rows = val[24 * o:24 * o + 24, :]
            chunk = jnp.concatenate([rows[:, 384 * k:384 * (k + 1)] for k in range(nb)], 0)
            dst[cc, 2 * b + zz, xx] = chunk.astype(BF16)

    def ff_bwd(l):
        s = 2 * l + 1
        row = lambda ref: ref[pl.ds(l, 1), :]
        sg, dbg = head_back(s, row(fsc))
        v0[l, 3:4, :] = sg
        v0[l, 2:3, :] = dbg
        g = br[s]
        for j in range(4):
            c = slice(D * j, D * (j + 1))
            ga = dot_rt(g, w_dn[c, :])
            gbef = (ga * dg[:, c].astype(F32)).astype(BF16)
            dg[:, c] = gbef
            v0[l, 4 + j:5 + j, :] = rowsum(fold8(gbef.astype(F32)))
        @pl.when(l == 0)
        def _():
            cm.step(3, 0, 1)
        @pl.when(y < 2)
        def _():
            def b2(b, _):
                a = low[s, :, pl.ds(pl.multiple_of(b * 384, 128), 384)]
                put_rows(fch, b, dot_lt(a, dg[:, pl.ds(pl.multiple_of(y * 1536, 128), 1536)]), 4)
                return 0
            lax.fori_loop(0, 2, b2, 0)
        @pl.when(y >= 2)
        def _():
            gq = br[s, :, pl.ds(pl.multiple_of((y - 2) * 384, 128), 384)]
            def b4(zz, _):
                a = af[:, pl.ds(pl.multiple_of(zz * 768, 128), 768)]
                val = dot_lt(a, gq).astype(BF16)
                for o in range(8):
                    fch[o % 2, zz, o // 2] = val[96 * o:96 * o + 96, :]
                return 0
            lax.fori_loop(0, 4, b4, 0)
        cm.c_start(0, l)
        for j in range(2):
            T[0, 256 * j:256 * j + 256] = dot_rt(dg[256 * j:256 * j + 256], w_up[...])
        @pl.when(l == 0)
        def _():
            cm.step(2, 1, 1)
        @pl.when(l == 1)
        def _():
            c_so.wait()
        gg, sh = tail_back(s, row(fg))
        v0[l, 0:1, :] = gg
        v0[l, 1:2, :] = sh

    def attn_bwd(l):
        s = 2 * l
        row = lambda ref: ref[pl.ds(l, 1), :]
        sg, obg = head_back(s, row(asc))

        def small(i, val):
            @pl.when(l == 1)
            def _():
                v0[2, i:i + 1, :] = val
            @pl.when(l == 0)
            def _():
                if i < 2:
                    v2[i:i + 1, :] = val
                else:
                    v0[3, i:i + 1, :] = val
        small(5, sg)
        small(4, obg)
        cm.step(1, 0, l)
        low[s + 1] = dot_rt(br[s], w_out[...]).astype(BF16)
        T[...] = jnp.zeros_like(T)

        def pair(mb, g):
            it = 6 * mb + g
            rows, cols, q, km, vm = masks(g, mb, l)
            dop = low[s + 1, rows, cols]
            dp = dot_rt(vm, dop)
            e = E[it]
            ef = e.astype(F32)
            pt = ef * dp
            in0 = jnp.sum(pt[:MB], 0, keepdims=True) / jnp.sum(ef[:MB], 0, keepdims=True)
            in1 = jnp.sum(pt[MB:], 0, keepdims=True) / jnp.sum(ef[MB:], 0, keepdims=True)
            ds = jnp.concatenate([pt[:MB] - ef[:MB] * in0, pt[MB:] - ef[MB:] * in1], 0).astype(BF16)
            for k in range(2):
                b = head_block(2 * g + k)
                T[b] = T[b] + ds[MB * k:MB * k + MB].astype(F32)
            dv = dot(e, dop)
            dk = dot(ds, q)
            dq = (dot_lt(km, ds) * 0.125).T
            hm = lane < 64
            c0 = pl.multiple_of(g * 128, 128)
            qkv[l, rows, pl.ds(c0, 128)] = dq.astype(BF16)
            qkv[l, rows, pl.ds(D + c0, 128)] = jnp.where(hm, dk[:MB], dk[MB:]).astype(BF16)
            qkv[l, rows, pl.ds(2 * D + c0, 128)] = jnp.where(hm, dv[:MB], dv[MB:]).astype(BF16)

        for g in range(6):
            pair(0, g)

        @pl.when(l == 0)
        def _():
            cm.step(3, 1, 1)
        for g in range(6):
            pair(1, g)
        @pl.when(y < 3)
        def _():
            def b2(b, _):
                a = low[s, :, pl.ds(pl.multiple_of(b * 384, 128), 384)]
                put_rows(ach, b, dot_lt(a, qkv[l, :, pl.ds(pl.multiple_of(y * D, 128), D)]), 2)
                return 0
            lax.fori_loop(0, 2, b2, 0)
        @pl.when(y == 3)
        def _():
            def b2(b, _):
                a = mixed[l, :, pl.ds(pl.multiple_of(b * 384, 128), 384)]
                put_rows(ach, b, dot_lt(a, br[s]), 2)
                return 0
            lax.fori_loop(0, 2, b2, 0)
        cm.c_start(1, l)
        def cs(i, c):
            a, b = c
            r = pl.ds(pl.multiple_of(i * 64, 64), 64)
            return a + fold8(qkv[l, r, 0:D].astype(F32)), b + fold8(qkv[l, r, 2 * D:3 * D].astype(F32))
        z = jnp.zeros((8, D), F32)
        a, b = lax.fori_loop(0, R // 64, cs, (z, z), unroll=UL)
        small(2, rowsum(a))
        small(3, rowsum(b))
        @pl.when(l == 0)
        def _():
            cm.v_start(0, 0)
        def fo(h, _):
            h = 3 * y + h
            a = T[head_block(h)]
            a = jnp.concatenate([a, jnp.zeros((MB, MB), F32)], 1)
            n = MB // 2
            while n >= 1:
                a = a[n:, :] + pltpu.roll(a[:n, :], n, 1)
                n //= 2
            Dsc[pl.ds(h, 1), :] = a
            return 0
        with jax.named_scope('fold'):
            lax.fori_loop(0, 3, fo, 0, unroll=True)
        tg = lax.dot_general(Dsc[...], sel, (((1,), (1,)), ((), ())), precision=lax.Precision.HIGHEST, preferred_element_type=F32)
        v3[pl.ds(pl.multiple_of(l * 16, 16), 16), :] = jnp.concatenate([tg, jnp.zeros((16, 96), F32)], 1)
        @pl.when(l == 0)
        def _():
            cm.v_start(2, 0)
            cm.v_start(0, 1)
        T[0] = dot_rt(qkv[l], w_in[...])
        cm.step(1, 1, l)
        @pl.when(l == 0)
        def _():
            cm.v_start(2, 1)
        cm.step(2, 0, l)
        gg, sh = tail_back(s, row(ag))
        small(0, gg)
        small(1, sh)

    v0[...] = jnp.zeros_like(v0)
    Dsc[...] = jnp.zeros_like(Dsc)

    def bwd(i, _):
        l = 1 - i
        @pl.when(l == 0)
        def _():
            wait(ldF(0))
            wait([cp(af_st, af, 7), cp(dg_st, dg, 8)])
        ff_bwd(l)
        @pl.when(l == 1)
        def _():
            start(ldF(0))
            start([cp(af_st, af, 7), cp(dg_st, dg, 8)])
        @pl.when(l == 0)
        def _():
            wait(ldA(0))
            wait([cp(e_st, E, 6)])
        attn_bwd(l)
        @pl.when(l == 1)
        def _():
            start(ldA(0))
            cp(e_st, E, 6).start()
        return 0
    lax.fori_loop(0, 2, bwd, 0)
    cm.v_start(1, 0)
    cm.v_start(0, 2)
    cm.v_start(2, 2)
    cm.v_start(1, 1)
    cm.step(2, 1, 0)
    cm.step(3, 0, 0)
    cm.v_start(0, 3)
    cm.v_start(2, 3)
    cm.v_start(1, 2)
    cm.step(3, 1, 0)
    cm.v_finish(0, 3)
    cm.v_finish(2, 3)
    cm.v_finish(1, 2)
    cp(xs.at[y], go, 10).wait()
    for l in (1, 0):
        for k in range(2):
            cm.y_done(k, l)


def run_chain(tokens, cotangent, pages, bucket, ag, ash, win, qb, vb, tab, wout, ob, asc, fg, fsh, wup, ub, wdn, db, fsc):
    tok = tokens.reshape(R, D)
    cot = cotangent.reshape(R, D)
    bucket = bucket.reshape(1, 511)
    tab = jnp.transpose(tab, (1, 0, 2))
    ANY = pl.BlockSpec(memory_space=pl.ANY)
    V = pl.BlockSpec(memory_space=pltpu.VMEM)
    sds = jax.ShapeDtypeStruct
    outs = (sds((R, D), BF16), sds((R, D), BF16), sds((4, 288, 384), BF16), sds((4, 8, D), F32), sds((2, D), F32), sds((32, 128), F32),
            sds((12, 512, MB), BF16), sds((R, FF), BF16), sds((R, FF), BF16))
    vm = pltpu.VMEM
    S = pltpu.SemaphoreType.DMA
    scratch = [
        vm((6, R, D), BF16), vm((4, R, D), BF16), vm((2, R, 3 * D), BF16), vm((12, 512, MB), BF16),
        vm((2, R, D), BF16), vm((4, R, D), BF16), vm((R, FF), BF16), vm((R, FF), BF16),
        vm((D, 3 * D), BF16), vm((D, D), BF16), vm((D, FF), BF16), vm((FF, D), BF16),
        vm((2, R, D), F32),
        vm((2, 2, MB, 128), BF16), vm((16, 512), F32), vm((1, 512), jnp.int32), vm((2, 4, 4, 96, 384), BF16), vm((2, 4, 4, 48, 384), BF16),
        vm((4, 4, 144, 384), BF16), vm((3, 4, 288, 384), BF16), vm((3, 288, 384), BF16),
        vm((10, 8, D), F32), vm((7, 2, D), F32), vm((10, 32, 128), F32),
        S((11,)), S((4, 4, 6)), S((4, 4, 6)), S((3, 10)), S((3, 10)), pltpu.SemaphoreType.REGULAR((2,)),
    ]
    return pl.pallas_call(
        chain,
        out_shape=outs,
        in_specs=[ANY, ANY, V, V, V, V, ANY, V, V, V, ANY, V, V, V, V, ANY, V, ANY, V, V],
        out_specs=(ANY, ANY, V, V, V, V, ANY, ANY, ANY),
        scratch_shapes=scratch,
        compiler_params=pltpu.CompilerParams(vmem_limit_bytes=63400000, collective_id=0, has_side_effects=True),
        name="chain",
    )(tok, cot, pages, bucket, ag, ash, win, qb, vb, tab, wout, ob, asc, fg, fsh, wup, ub, wdn, db, fsc)


def unpack(so_in, go_in, G_in, v0_in, v2_in, v3_in, so, go, a_gain, a_shift, w_in, qb, vb, tab, w_out, ob, asc, fg, fsh, w_up, ub, w_dn, db, fsc, G, v0, v2, v3, so_mid, go_mid, sem):
    d = lax.axis_index("dp")
    pairs = ((so_in, so_mid), (go_in, go_mid), (G_in, G), (v0_in, v0), (v2_in, v2), (v3_in, v3))
    copies = [pltpu.make_async_copy(a, b, sem.at[i]) for i, (a, b) in enumerate(pairs)]
    for cp in copies:
        cp.start()
    last = [pltpu.make_async_copy(a, b, sem.at[6 + i]) for i, (a, b) in enumerate(((so_mid, so), (go_mid, go)))]
    for a, b in zip(copies[:2], last):
        a.wait()
        b.start()
    for cp in copies[2:]:
        cp.wait()
    for l in range(2):
        for y in range(4):
            f = G[y, 96 * l:96 * l + 96, :].astype(F32)
            a = G[y, 192 + 48 * l:240 + 48 * l, :].astype(F32)
            if y < 2:
                for k in range(4):
                    w_up[l, :, 1536 * y + 384 * k:1536 * y + 384 * (k + 1)] = f[24 * k:24 * k + 24]
            else:
                w_dn[l, :, 384 * (y - 2):384 * (y - 1)] = f
            for k in range(2):
                if y < 3:
                    w_in[l, :, 768 * y + 384 * k:768 * y + 384 * (k + 1)] = a[24 * k:24 * k + 24]
                else:
                    w_out[l, :, 384 * k:384 * (k + 1)] = a[24 * k:24 * k + 24]
    shift = lax.rem(D - 24 * d, D)
    r0 = [pltpu.roll(v0[i], shift, 1)[:, :128] for i in range(4)]
    r2 = pltpu.roll(jnp.concatenate([v2[...], jnp.zeros((6, D), F32)], 0), shift, 1)[:, :128]
    for i, ref in enumerate((fg, fsh, db, fsc)):
        for l in range(2):
            ref[l:l + 1, :] = r0[l][i:i + 1, :24]
    for i, ref in enumerate((a_gain, a_shift, qb, vb, ob, asc)):
        ref[1:2, :] = r0[2][i:i + 1, :24]
        ref[0:1, :] = (r2 if i < 2 else r0[3])[i:i + 1, :24]
    for l in range(2):
        row = v0[l, pl.ds(4 + d // 8, 1), :]
        ub[l:l + 1, :] = pltpu.roll(jnp.broadcast_to(row, (8, D)), lax.rem(D - 96 * lax.rem(d, 8), D), 1)[0:1, :96]
        tab[:, l, :] = v3[16 * l:16 * l + H, :NB]
    for cp in last:
        cp.wait()


def run_unpack(*args):
    V = pl.BlockSpec(memory_space=pltpu.VMEM)
    ANY = pl.BlockSpec(memory_space=pl.ANY)
    sds = jax.ShapeDtypeStruct
    w = sds((2, 24), F32)
    outs = (sds((R, D), BF16), sds((R, D), BF16), w, w, sds((2, 24, 2304), F32), w, w, sds((H, 2, NB), F32), sds((2, 24, D), F32), w, w, w, w,
            sds((2, 24, FF), F32), sds((2, 96), F32), sds((2, 96, D), F32), w, w)
    vm = pltpu.VMEM
    return pl.pallas_call(
        unpack, out_shape=outs, in_specs=[ANY] * 6, out_specs=(ANY, ANY) + (V,) * 16, name="unpack",
        scratch_shapes=[vm((4, 288, 384), BF16), vm((4, 8, D), F32), vm((2, D), F32), vm((32, 128), F32), vm((R, D), BF16), vm((R, D), BF16), pltpu.SemaphoreType.DMA((8,))],
        compiler_params=pltpu.CompilerParams(vmem_limit_bytes=63400000))(*args)


def body(*args):
    so, go, *outs = run_unpack(*run_chain(*args)[:6])
    outs[5] = jnp.transpose(outs[5], (1, 0, 2))
    return (so.reshape(1, 2, MB, D), go.reshape(1, 2, MB, D)) + tuple(outs)


def solution(mesh):
    data, whole = P("dp", None, None), P()
    w1, w2 = P(None, "dp"), P(None, "dp", None)
    return jax.shard_map(
        body,
        mesh=mesh,
        in_specs=(data, data, P("dp", None)) + (whole,) * 17,
        out_specs=(P("section", "dp", None, None),) * 2 + (w1, w1, w2, w1, w1, P(), w2, w1, w1, w1, w1, w2, w1, w2, w1, w1),
        check_vma=False,
    )
```

```python
import functools
import jax
import jax.numpy as jnp
from jax import lax
from jax.experimental import pallas as pl
from jax.experimental.pallas import tpu as pltpu
from jax.sharding import PartitionSpec as P

D, H, HD, FF, NB, MB = 768, 12, 64, 3072, 32, 256
R = 512
EPS = 1e-5
UP, UL = 12, 8
F32, BF16 = jnp.float32, jnp.bfloat16
C0 = 0.7978845608028654
C1 = 0.044715 * C0


def dot(a, b):
    return jnp.dot(a, b, preferred_element_type=F32)


def dot_rt(a, b):
    return lax.dot_general(a, b, (((1,), (1,)), ((), ())), preferred_element_type=F32)


def dot_lt(a, b):
    return lax.dot_general(a, b, (((0,), (0,)), ((), ())), preferred_element_type=F32)


def fold8(v):
    return jnp.sum(v.reshape(v.shape[0] // 8, 8, v.shape[1]), axis=0)


def rowsum(v):
    return jnp.sum(v, axis=0, keepdims=True)


MESH = pl.DeviceIdType.MESH
KINDS = ((96, 48, 0, 0), (48, 32, 192, 96))


class Comm:
    def __init__(self, vecs, fch, ach, rc, rx1, rx2, G, vxs, sems, semr, vsems, vsemr, credit):
        d = lax.axis_index("dp")
        self.y = lax.axis_index("section")
        self.z, self.x, self.c = d // 8, lax.rem(d // 2, 4), lax.rem(d, 2)
        self.vecs, self.own, self.rc, self.G, self.vxs = vecs, (fch, ach), rc, G, vxs
        self.rx1, self.rx2 = rx1, rx2
        self.sems, self.semr, self.vsems, self.vsemr, self.credit = sems, semr, vsems, vsemr, credit

    def dev(self, axis, o):
        at = {"z": self.z, "x": self.x, "c": self.c, "y": self.y}
        at[axis] = o
        return (at["z"] * 8 + at["x"] * 2 + at["c"], at["y"])

    def others(self, axis):
        me = getattr(self, axis)
        if axis == "c":
            return [(1 - me, 0, 0)]
        return [(lax.rem(me + i, 4), 3 - i, i - 1) for i in (2, 1, 3)]

    def signal_all(self):
        b = pltpu.get_barrier_semaphore()
        for axis in "cxzy":
            for o, _, _ in self.others(axis):
                pl.semaphore_signal(b, inc=1, device_id=self.dev(axis, o), device_id_type=MESH)

    def wait_all(self):
        pl.semaphore_wait(pltpu.get_barrier_semaphore(), 10)

    def copy(self, src, dst, sem, device):
        return pltpu.make_async_remote_copy(src_ref=src, dst_ref=dst, send_sem=self.sems.at[sem], recv_sem=self.semr.at[sem],
                                            device_id=device, device_id_type=MESH)

    def rows(self, kind, l, lo, m):
        n, _, g, _ = KINDS[kind]
        return pl.ds(lo, m), pl.ds(pl.multiple_of(g + n * l + lo, 16), m)

    def half(self, kind, h):
        n, a, _, _ = KINDS[kind]
        return (0, a) if h == 0 else (a, n - a)

    def unit(self, kind, l):
        return 2 * (1 - l) + kind

    def c_copy(self, kind, l):
        n, _, _, r = KINDS[kind]
        o = 1 - self.c
        return self.copy(self.own[kind].at[o], self.rc.at[:, :, r:r + n, :], (self.unit(kind, l), 0, 0), self.dev("c", o))

    def c_start(self, kind, l):
        @pl.when(l == 0)
        def _():
            pl.semaphore_wait(self.credit.at[kind], 1)
        self.c_copy(kind, l).start()

    def at(self, kind, axis, i, j, rows):
        own = self.own[kind]
        return own.at[self.c, j, i, rows, :] if axis == "x" else own.at[self.c, i, j, rows, :]

    def hops(self, kind, l, phase):
        out = []
        u = self.unit(kind, l)
        for h in range(2):
            axis, first = ("xz"[h], None) if phase == 1 else ("zx"[h], "xz"[h])
            me = getattr(self, axis)
            mine, every = self.rows(kind, l, *self.half(kind, h))
            j = pl.ds(0, 4) if phase == 1 else getattr(self, first)
            buf = self.rx1 if phase == 1 else self.rx2
            for o, there, here in self.others(axis):
                cps = []
                for slot in (there, here):
                    dst = buf.at[slot, :, every, :] if phase == 1 else buf.at[slot, every, :]
                    cps.append(self.copy(self.at(kind, axis, o, j, mine), dst, (u, phase, 3 * h + slot), self.dev(axis, o)))
                out.append((h, cps[0], cps[1]))
        return out

    def launch(self, kind, l, phase):
        for _, cp, _ in self.hops(kind, l, phase):
            cp.start()

    def land(self, kind, l, phase):
        hops = self.hops(kind, l, phase)
        for h in range(2):
            for hh, _, cp in hops:
                if hh == h:
                    cp.wait_recv()
            axis = "xz"[h] if phase == 1 else "zx"[h]
            me = getattr(self, axis)
            mine, every = self.rows(kind, l, *self.half(kind, h))

            def total(s, parts):
                v = s[...].astype(F32)
                for p in parts:
                    v = v + p.astype(F32)
                s[...] = v.astype(BF16)
            if phase == 1:
                def add(i, _):
                    total(self.at(kind, axis, me, i, mine), [self.rx1[k, i, every, :] for k in range(3)])
                    return 0
                lax.fori_loop(0, 4, add, 0)
            else:
                total(self.at(kind, axis, me, getattr(self, "xz"[h]), mine), [self.rx2[k, every, :] for k in range(3)])
        for _, cp, _ in hops:
            cp.wait_send()

    def step(self, i, kind, l):
        if i == 1:
            n, _, _, r = KINDS[kind]
            own, c = self.own[kind], self.c
            cc = self.c_copy(kind, l)
            cc.wait_recv()

            def add(i, _):
                z, x = i // 4, lax.rem(i, 4)
                own[c, z, x] = (own[c, z, x].astype(F32) + self.rc[z, x, r:r + n, :].astype(F32)).astype(BF16)
                return 0
            lax.fori_loop(0, 16, add, 0)

            @pl.when(l == 1)
            def _():
                pl.semaphore_signal(self.credit.at[kind], inc=1, device_id=self.dev("c", 1 - c), device_id_type=MESH)
            self.launch(kind, l, 1)
            cc.wait_send()
        elif i == 2:
            self.land(kind, l, 1)
            self.launch(kind, l, 2)
        else:
            self.land(kind, l, 2)
            n = KINDS[kind][0]
            _, every = self.rows(kind, l, 0, n)
            self.G[self.y, every, :] = self.own[kind][self.c, self.z, self.x]
            for o, there, _ in self.others("y"):
                self.y_copy(kind, l, o, self.y, there).start()

    def y_copy(self, kind, l, o, slot, there):
        _, every = self.rows(kind, l, 0, KINDS[kind][0])
        part = self.G.at[slot, every, :]
        return self.copy(part, part, (self.unit(kind, l), 3, there), self.dev("y", o))

    def y_done(self, kind, l):
        for o, there, here in self.others("y"):
            self.y_copy(kind, l, o, o, here).wait_recv()
            self.y_copy(kind, l, o, self.y, there).wait_send()

    def vec(self, b):
        return self.vecs[0].at[self.y] if b == 0 else self.vecs[b]

    def v_copy(self, b, stage, o, there):
        i = (0, 1, 4, 7)[stage] + there
        src = self.vec(b)
        dst = self.vxs[b].at[i]
        return pltpu.make_async_remote_copy(src_ref=src, dst_ref=dst, send_sem=self.vsems.at[b, i], recv_sem=self.vsemr.at[b, i],
                                            device_id=self.dev("cxzy"[stage], o), device_id_type=MESH)

    def v_start(self, b, stage):
        if stage:
            self.v_finish(b, stage - 1)
        for o, there, _ in self.others("cxzy"[stage]):
            self.v_copy(b, stage, o, there).start()

    def v_finish(self, b, stage):
        axis = "cxzy"[stage]
        me = getattr(self, axis)
        vec, vx = self.vec(b), self.vxs[b]
        for o, there, here in self.others(axis):
            self.v_copy(b, stage, o, here).wait_recv()
            self.v_copy(b, stage, o, there).wait_send()
            if b == 0 and stage == 3:
                self.vecs[0][o] = vx[7 + here]
        if b == 0 and stage == 3:
            return
        if stage == 0:
            vec[...] = vec[...] + vx[0]
            return
        own = vec[...]
        terms = []
        for p in range(4):
            slot = lax.rem(p - me + 7, 4)
            terms.append(jnp.where(slot == 3, own, vx[(1, 4, 7)[stage - 1] + jnp.minimum(slot, 2)]))
        vec[...] = (terms[0] + terms[1]) + (terms[2] + terms[3])


def head_block(h):
    k = h % 6
    if isinstance(h, int):
        return h // 6, slice(MB * (k // 3), MB * (k // 3) + MB), slice(MB * (k % 3), MB * (k % 3) + MB)
    return h // 6, pl.ds(pl.multiple_of(MB * (k // 3), MB), MB), pl.ds(pl.multiple_of(MB * (k % 3), MB), MB)


def chain(tok, cot, pages, bucket, ag, ash, win, qb, vb, tab, wout, ob, asc, fg, fsh, wup, ub, wdn, db, fsc,
       so, go, G, v0, v2, v3, e_st, af_st, dg_st,
       xs, low, qkv, E, mixed, br, af, dg, w_in, w_out, w_up, w_dn, T, AB, Dsc, bsc, fch, ach,
       rc, rx1, rx2, vx0, vx2, vx3, sem, sems, semr, vsems, vsemr, credit):
    cm = Comm((v0, v2, v3), fch, ach, rc, rx1, rx2, G, (vx0, vx2, vx3), sems, semr, vsems, vsemr, credit)
    y = cm.y
    def cp(src, dst, i):
        return pltpu.make_async_copy(src, dst, sem.at[i])
    def ldA(l):
        return [cp(win.at[l], w_in, 0), cp(wout.at[l], w_out, 1)]
    def ldF(l):
        return [cp(wup.at[l], w_up, 2), cp(wdn.at[l], w_dn, 3)]
    def start(cs):
        for c in cs: c.start()
    def wait(cs):
        for c in cs: c.wait()
    ctok = cp(tok, xs.at[0], 4)
    ccot = cp(cot, xs.at[5], 5)
    ctok.start()
    start(ldA(0))
    start(ldF(0))
    ccot.start()
    cm.signal_all()
    bsc[...] = jnp.full((1, 512), -1, jnp.int32)
    bsc[:, :511] = bucket[...]
    lane = lax.broadcasted_iota(jnp.int32, (1, 128), 1)
    m0 = (lane < 64).astype(F32).astype(BF16)
    m1 = (lane >= 64).astype(F32).astype(BF16)
    lanef = lax.broadcasted_iota(jnp.int32, (MB, 128), 1).astype(F32)
    for mb in range(2):
        pf = jnp.broadcast_to(pages[mb:mb + 1, :].astype(F32), (128, MB)).T
        same = pf == lanef
        AB[0, mb] = jnp.where(same | (lanef > 7.5), 0.0, -1e30).astype(BF16)
        AB[1, mb] = jnp.where(same, 1.0, 0.0).astype(BF16)
    turn = (lax.broadcasted_iota(jnp.int32, (512, 512), 0) + lax.broadcasted_iota(jnp.int32, (512, 512), 1) == 510).astype(F32).astype(BF16)
    turned = dot(jnp.broadcast_to(bsc[...].astype(F32), (16, 512)).astype(BF16), turn)[0:1, :]
    turned = jnp.where(lax.broadcasted_iota(jnp.int32, (1, 512), 1) == 511, -1.0, turned)
    sel = (lax.broadcasted_iota(jnp.int32, (NB, 512), 0).astype(F32) == turned).astype(F32)

    def layernorm(s, gain, shift):
        def body(i, _):
            r = pl.ds(pl.multiple_of(i * 64, 64), 64)
            x = xs[s, r, :].astype(F32)
            c = x - jnp.mean(x, -1, keepdims=True)
            n = c * lax.rsqrt(jnp.mean(c * c, -1, keepdims=True) + EPS)
            low[s, r, :] = (n * gain + shift).astype(BF16)
            return 0
        lax.fori_loop(0, R // 64, body, 0, unroll=UL)

    def residual(s, val, bias, scale):
        b = val + bias
        br[s] = b.astype(BF16)
        xs[s + 1] = (xs[s].astype(F32) + scale * b).astype(BF16)

    def masks(g, mb, l):
        rows = pl.ds(pl.multiple_of(mb * MB, MB), MB)
        c = pl.multiple_of(g * 128, 128)
        q = qkv[l, rows, pl.ds(c, 128)]
        k = qkv[l, rows, pl.ds(D + c, 128)]
        v = qkv[l, rows, pl.ds(2 * D + c, 128)]
        km = jnp.concatenate([k * m0, k * m1], 0)
        vm = jnp.concatenate([v * m0, v * m1], 0)
        return rows, pl.ds(c, 128), q, km, vm

    def attn_fwd(l):
        s = 2 * l
        row = lambda ref: ref[pl.ds(l, 1), :]
        obias = lax.dot_general(tab[:, pl.ds(l, 1), :].reshape(H, NB), sel, (((1,), (0,)), ((), ())), precision=lax.Precision.HIGHEST, preferred_element_type=F32)
        def toep():
            base = [pltpu.roll(jnp.broadcast_to(obias[h:h + 1, :], (8, 512)), 257, 1, stride=1, stride_axis=0) for h in range(H)]
            base = jnp.concatenate(base, 0)
            for a in range(MB // 8):
                t = pltpu.roll(base, 8 * a, 1) if a else base
                for h in range(H):
                    p, r, c = head_block(h)
                    T[p, r.start + 8 * a:r.start + 8 * a + 8, c] = t[8 * h:8 * h + 8, :MB]
        with jax.named_scope('toep'):
            toep()
        layernorm(s, row(ag), row(ash))
        x = low[s]
        qkv[l, :, 0:D] = ((dot(x, w_in[:, 0:D]) + row(qb)) * 0.125).astype(BF16)
        qkv[l, :, D:2 * D] = dot(x, w_in[:, D:2 * D]).astype(BF16)
        qkv[l, :, 2 * D:3 * D] = (dot(x, w_in[:, 2 * D:3 * D]) + row(vb)).astype(BF16)
        def pair(it, _):
            mb, g = it // 6, it % 6
            rows, cols, q, km, vm = masks(g, mb, l)
            qx = jnp.concatenate([q, AB[0, mb]], 1)
            kx = jnp.concatenate([km, jnp.concatenate([AB[1, mb]] * 2, 0)], 1)
            sc = dot_rt(kx, qx)
            def soft(v):
                e = jnp.exp(v - jnp.max(v, 0, keepdims=True))
                return e * (1.0 / jnp.sum(e, 0, keepdims=True))
            e = jnp.concatenate([soft(sc[:MB] + T[head_block(2 * g)]), soft(sc[MB:] + T[head_block(2 * g + 1)])], 0).astype(BF16)
            E[it] = e
            mixed[l, rows, cols] = dot_lt(vm, e).T.astype(BF16)
            return 0
        with jax.named_scope('pairs'):
            lax.fori_loop(0, 12, pair, 0, unroll=UP)
        residual(s, dot(mixed[l], w_out[...]), row(ob), row(asc))

    def ff_fwd(l):
        s = 2 * l + 1
        row = lambda ref: ref[pl.ds(l, 1), :]
        layernorm(s, row(fg), row(fsh))
        x = low[s]
        for j in range(4):
            u = dot(x, w_up[:, D * j:D * (j + 1)]) + ub[pl.ds(l, 1), D * j:D * (j + 1)]
            u2 = u * u
            t = jnp.tanh(u * (C0 + C1 * u2))
            h = 0.5 * t + 0.5
            af[:, D * j:D * (j + 1)] = (u * h).astype(BF16)
            dg[:, D * j:D * (j + 1)] = (h + (0.5 - 0.5 * t * t) * (u * (C0 + (3 * C1) * u2))).astype(BF16)
        for j in range(2):
            r = slice(256 * j, 256 * j + 256)
            b = dot(af[r], w_dn[...]) + row(db)
            br[s, r] = b.astype(BF16)
            xs[s + 1, r] = (xs[s, r].astype(F32) + row(fsc) * b).astype(BF16)

    def fwd(l, _):
        @pl.when(l == 1)
        def _():
            wait([cp(E, e_st, 6)])
        wait(ldA(l))
        attn_fwd(l)
        @pl.when(l == 0)
        def _():
            start(ldA(1))
            cp(E, e_st, 6).start()
        @pl.when(l == 1)
        def _():
            wait([cp(af, af_st, 7), cp(dg, dg_st, 8)])
        wait(ldF(l))
        ff_fwd(l)
        @pl.when(l == 0)
        def _():
            start(ldF(1))
            start([cp(af, af_st, 7), cp(dg, dg_st, 8)])
        return 0

    ctok.wait()
    lax.fori_loop(0, 2, fwd, 0)
    c_so = cp(xs.at[y + 1], so, 9)
    c_so.start()
    ccot.wait()
    cm.wait_all()

    def up_slot(s):
        return jnp.where(s == 3, 5, s + 1)

    def head_back(s, scale):
        us = up_slot(s)

        def body(i, c):
            a, b = c
            r = pl.ds(pl.multiple_of(i * 64, 64), 64)
            u = xs[us, r, :].astype(F32)
            g = (u * scale).astype(BF16)
            b8 = fold8(u * br[s, r, :].astype(F32))
            br[s, r, :] = g
            return a + b8, b + fold8(g.astype(F32))
        z = jnp.zeros((8, D), F32)
        a, b = lax.fori_loop(0, R // 64, body, (z, z), unroll=UL)
        return rowsum(a), rowsum(b)

    def tail_back(s, gain):
        us = up_slot(s)

        def body(i, c):
            a, b = c
            r = pl.ds(pl.multiple_of(i * 64, 64), 64)
            x = xs[s, r, :].astype(F32)
            gl = T[0, r, :]
            ce = x - jnp.mean(x, -1, keepdims=True)
            rs = lax.rsqrt(jnp.mean(ce * ce, -1, keepdims=True) + EPS)
            n = ce * rs
            gn = gl * n
            t = gl * gain
            u = xs[us, r, :].astype(F32)
            o = u + rs * (t - jnp.mean(t, -1, keepdims=True) - n * jnp.mean(t * n, -1, keepdims=True))
            xs[s, r, :] = o.astype(BF16)
            return a + fold8(gn), b + fold8(gl)
        z = jnp.zeros((8, D), F32)
        a, b = lax.fori_loop(0, R // 64, body, (z, z), unroll=UL)
        @pl.when(y == s)
        def _():
            cp(xs.at[s], go, 10).start()
        return rowsum(a), rowsum(b)

    def put_rows(dst, b, val, nb):
        for o in range(16):
            zz, xx, cc = o // 8, (o // 2) % 4, o % 2
            rows = val[24 * o:24 * o + 24, :]
            chunk = jnp.concatenate([rows[:, 384 * k:384 * (k + 1)] for k in range(nb)], 0)
            dst[cc, 2 * b + zz, xx] = chunk.astype(BF16)

    def ff_bwd(l):
        s = 2 * l + 1
        row = lambda ref: ref[pl.ds(l, 1), :]
        sg, dbg = head_back(s, row(fsc))
        v0[l, 3:4, :] = sg
        v0[l, 2:3, :] = dbg
        g = br[s]
        for j in range(4):
            c = slice(D * j, D * (j + 1))
            ga = dot_rt(g, w_dn[c, :])
            gbef = (ga * dg[:, c].astype(F32)).astype(BF16)
            dg[:, c] = gbef
            v0[l, 4 + j:5 + j, :] = rowsum(fold8(gbef.astype(F32)))
        @pl.when(l == 0)
        def _():
            cm.step(3, 0, 1)
        @pl.when(y < 2)
        def _():
            def b2(b, _):
                a = low[s, :, pl.ds(pl.multiple_of(b * 384, 128), 384)]
                put_rows(fch, b, dot_lt(a, dg[:, pl.ds(pl.multiple_of(y * 1536, 128), 1536)]), 4)
                return 0
            lax.fori_loop(0, 2, b2, 0)
        @pl.when(y >= 2)
        def _():
            gq = br[s, :, pl.ds(pl.multiple_of((y - 2) * 384, 128), 384)]
            def b4(zz, _):
                a = af[:, pl.ds(pl.multiple_of(zz * 768, 128), 768)]
                val = dot_lt(a, gq).astype(BF16)
                for o in range(8):
                    fch[o % 2, zz, o // 2] = val[96 * o:96 * o + 96, :]
                return 0
            lax.fori_loop(0, 4, b4, 0)
        cm.c_start(0, l)
        for j in range(2):
            T[0, 256 * j:256 * j + 256] = dot_rt(dg[256 * j:256 * j + 256], w_up[...])
        @pl.when(l == 0)
        def _():
            cm.step(2, 1, 1)
        @pl.when(l == 1)
        def _():
            c_so.wait()
        gg, sh = tail_back(s, row(fg))
        v0[l, 0:1, :] = gg
        v0[l, 1:2, :] = sh

    def attn_bwd(l):
        s = 2 * l
        row = lambda ref: ref[pl.ds(l, 1), :]
        sg, obg = head_back(s, row(asc))

        def small(i, val):
            @pl.when(l == 1)
            def _():
                v0[2, i:i + 1, :] = val
            @pl.when(l == 0)
            def _():
                if i < 2:
                    v2[i:i + 1, :] = val
                else:
                    v0[3, i:i + 1, :] = val
        small(5, sg)
        small(4, obg)
        cm.step(1, 0, l)
        low[s + 1] = dot_rt(br[s], w_out[...]).astype(BF16)
        T[...] = jnp.zeros_like(T)

        def pair(mb, g):
            it = 6 * mb + g
            rows, cols, q, km, vm = masks(g, mb, l)
            dop = low[s + 1, rows, cols]
            dp = dot_rt(vm, dop)
            e = E[it]
            ef = e.astype(F32)
            pt = ef * dp
            in0 = jnp.sum(pt[:MB], 0, keepdims=True) / jnp.sum(ef[:MB], 0, keepdims=True)
            in1 = jnp.sum(pt[MB:], 0, keepdims=True) / jnp.sum(ef[MB:], 0, keepdims=True)
            ds = jnp.concatenate([pt[:MB] - ef[:MB] * in0, pt[MB:] - ef[MB:] * in1], 0).astype(BF16)
            for k in range(2):
                b = head_block(2 * g + k)
                T[b] = T[b] + ds[MB * k:MB * k + MB].astype(F32)
            dv = dot(e, dop)
            dk = dot(ds, q)
            dq = (dot_lt(km, ds) * 0.125).T
            hm = lane < 64
            c0 = pl.multiple_of(g * 128, 128)
            qkv[l, rows, pl.ds(c0, 128)] = dq.astype(BF16)
            qkv[l, rows, pl.ds(D + c0, 128)] = jnp.where(hm, dk[:MB], dk[MB:]).astype(BF16)
            qkv[l, rows, pl.ds(2 * D + c0, 128)] = jnp.where(hm, dv[:MB], dv[MB:]).astype(BF16)

        for g in range(6):
            pair(0, g)

        @pl.when(l == 0)
        def _():
            cm.step(3, 1, 1)
        for g in range(6):
            pair(1, g)
        @pl.when(y < 3)
        def _():
            def b2(b, _):
                a = low[s, :, pl.ds(pl.multiple_of(b * 384, 128), 384)]
                put_rows(ach, b, dot_lt(a, qkv[l, :, pl.ds(pl.multiple_of(y * D, 128), D)]), 2)
                return 0
            lax.fori_loop(0, 2, b2, 0)
        @pl.when(y == 3)
        def _():
            def b2(b, _):
                a = mixed[l, :, pl.ds(pl.multiple_of(b * 384, 128), 384)]
                put_rows(ach, b, dot_lt(a, br[s]), 2)
                return 0
            lax.fori_loop(0, 2, b2, 0)
        cm.c_start(1, l)
        def cs(i, c):
            a, b = c
            r = pl.ds(pl.multiple_of(i * 64, 64), 64)
            return a + fold8(qkv[l, r, 0:D].astype(F32)), b + fold8(qkv[l, r, 2 * D:3 * D].astype(F32))
        z = jnp.zeros((8, D), F32)
        a, b = lax.fori_loop(0, R // 64, cs, (z, z), unroll=UL)
        small(2, rowsum(a))
        small(3, rowsum(b))
        @pl.when(l == 0)
        def _():
            cm.v_start(0, 0)
        def fo(h, _):
            h = 3 * y + h
            a = T[head_block(h)]
            a = jnp.concatenate([a, jnp.zeros((MB, MB), F32)], 1)
            n = MB // 2
            while n >= 1:
                a = a[n:, :] + pltpu.roll(a[:n, :], n, 1)
                n //= 2
            Dsc[pl.ds(h, 1), :] = a
            return 0
        with jax.named_scope('fold'):
            lax.fori_loop(0, 3, fo, 0, unroll=True)
        tg = lax.dot_general(Dsc[...], sel, (((1,), (1,)), ((), ())), precision=lax.Precision.HIGHEST, preferred_element_type=F32)
        v3[pl.ds(pl.multiple_of(l * 16, 16), 16), :] = jnp.concatenate([tg, jnp.zeros((16, 96), F32)], 1)
        @pl.when(l == 0)
        def _():
            cm.v_start(2, 0)
            cm.v_start(0, 1)
            cm.step(1, 1, 0)
        T[0] = dot_rt(qkv[l], w_in[...])
        @pl.when(l == 1)
        def _():
            cm.step(1, 1, 1)
        @pl.when(l == 0)
        def _():
            cm.v_start(2, 1)
        cm.step(2, 0, l)
        gg, sh = tail_back(s, row(ag))
        small(0, gg)
        small(1, sh)

    v0[...] = jnp.zeros_like(v0)
    Dsc[...] = jnp.zeros_like(Dsc)

    def bwd(i, _):
        l = 1 - i
        @pl.when(l == 0)
        def _():
            wait(ldF(0))
            wait([cp(af_st, af, 7), cp(dg_st, dg, 8)])
        ff_bwd(l)
        @pl.when(l == 1)
        def _():
            start(ldF(0))
            start([cp(af_st, af, 7), cp(dg_st, dg, 8)])
        @pl.when(l == 0)
        def _():
            wait(ldA(0))
            wait([cp(e_st, E, 6)])
        attn_bwd(l)
        @pl.when(l == 1)
        def _():
            start(ldA(0))
            cp(e_st, E, 6).start()
        return 0
    lax.fori_loop(0, 2, bwd, 0)
    cm.v_start(1, 0)
    cm.v_start(0, 2)
    cm.v_start(2, 2)
    cm.v_start(1, 1)
    cm.step(2, 1, 0)
    cm.step(3, 0, 0)
    cm.v_start(0, 3)
    cm.v_start(2, 3)
    cm.v_start(1, 2)
    cm.step(3, 1, 0)
    cm.v_finish(0, 3)
    cm.v_finish(2, 3)
    cm.v_finish(1, 2)
    cp(xs.at[y], go, 10).wait()
    for l in (1, 0):
        for k in range(2):
            cm.y_done(k, l)


def run_chain(tokens, cotangent, pages, bucket, ag, ash, win, qb, vb, tab, wout, ob, asc, fg, fsh, wup, ub, wdn, db, fsc):
    tok = tokens.reshape(R, D)
    cot = cotangent.reshape(R, D)
    bucket = bucket.reshape(1, 511)
    tab = jnp.transpose(tab, (1, 0, 2))
    ANY = pl.BlockSpec(memory_space=pl.ANY)
    V = pl.BlockSpec(memory_space=pltpu.VMEM)
    sds = jax.ShapeDtypeStruct
    outs = (sds((R, D), BF16), sds((R, D), BF16), sds((4, 288, 384), BF16), sds((4, 8, D), F32), sds((2, D), F32), sds((32, 128), F32),
            sds((12, 512, MB), BF16), sds((R, FF), BF16), sds((R, FF), BF16))
    vm = pltpu.VMEM
    S = pltpu.SemaphoreType.DMA
    scratch = [
        vm((6, R, D), BF16), vm((4, R, D), BF16), vm((2, R, 3 * D), BF16), vm((12, 512, MB), BF16),
        vm((2, R, D), BF16), vm((4, R, D), BF16), vm((R, FF), BF16), vm((R, FF), BF16),
        vm((D, 3 * D), BF16), vm((D, D), BF16), vm((D, FF), BF16), vm((FF, D), BF16),
        vm((2, R, D), F32),
        vm((2, 2, MB, 128), BF16), vm((16, 512), F32), vm((1, 512), jnp.int32), vm((2, 4, 4, 96, 384), BF16), vm((2, 4, 4, 48, 384), BF16),
        vm((4, 4, 144, 384), BF16), vm((3, 4, 288, 384), BF16), vm((3, 288, 384), BF16),
        vm((10, 8, D), F32), vm((7, 2, D), F32), vm((10, 32, 128), F32),
        S((11,)), S((4, 4, 6)), S((4, 4, 6)), S((3, 10)), S((3, 10)), pltpu.SemaphoreType.REGULAR((2,)),
    ]
    return pl.pallas_call(
        chain,
        out_shape=outs,
        in_specs=[ANY, ANY, V, V, V, V, ANY, V, V, V, ANY, V, V, V, V, ANY, V, ANY, V, V],
        out_specs=(ANY, ANY, V, V, V, V, ANY, ANY, ANY),
        scratch_shapes=scratch,
        compiler_params=pltpu.CompilerParams(vmem_limit_bytes=63400000, collective_id=0, has_side_effects=True),
        name="chain",
    )(tok, cot, pages, bucket, ag, ash, win, qb, vb, tab, wout, ob, asc, fg, fsh, wup, ub, wdn, db, fsc)


def unpack(so_in, go_in, G_in, v0_in, v2_in, v3_in, so, go, a_gain, a_shift, w_in, qb, vb, tab, w_out, ob, asc, fg, fsh, w_up, ub, w_dn, db, fsc, G, v0, v2, v3, so_mid, go_mid, sem):
    d = lax.axis_index("dp")
    pairs = ((so_in, so_mid), (go_in, go_mid), (G_in, G), (v0_in, v0), (v2_in, v2), (v3_in, v3))
    copies = [pltpu.make_async_copy(a, b, sem.at[i]) for i, (a, b) in enumerate(pairs)]
    for cp in copies:
        cp.start()
    last = [pltpu.make_async_copy(a, b, sem.at[6 + i]) for i, (a, b) in enumerate(((so_mid, so), (go_mid, go)))]
    for a, b in zip(copies[:2], last):
        a.wait()
        b.start()
    for cp in copies[2:]:
        cp.wait()
    for l in range(2):
        for y in range(4):
            f = G[y, 96 * l:96 * l + 96, :].astype(F32)
            a = G[y, 192 + 48 * l:240 + 48 * l, :].astype(F32)
            if y < 2:
                for k in range(4):
                    w_up[l, :, 1536 * y + 384 * k:1536 * y + 384 * (k + 1)] = f[24 * k:24 * k + 24]
            else:
                w_dn[l, :, 384 * (y - 2):384 * (y - 1)] = f
            for k in range(2):
                if y < 3:
                    w_in[l, :, 768 * y + 384 * k:768 * y + 384 * (k + 1)] = a[24 * k:24 * k + 24]
                else:
                    w_out[l, :, 384 * k:384 * (k + 1)] = a[24 * k:24 * k + 24]
    shift = lax.rem(D - 24 * d, D)
    r0 = [pltpu.roll(v0[i], shift, 1)[:, :128] for i in range(4)]
    r2 = pltpu.roll(jnp.concatenate([v2[...], jnp.zeros((6, D), F32)], 0), shift, 1)[:, :128]
    for i, ref in enumerate((fg, fsh, db, fsc)):
        for l in range(2):
            ref[l:l + 1, :] = r0[l][i:i + 1, :24]
    for i, ref in enumerate((a_gain, a_shift, qb, vb, ob, asc)):
        ref[1:2, :] = r0[2][i:i + 1, :24]
        ref[0:1, :] = (r2 if i < 2 else r0[3])[i:i + 1, :24]
    for l in range(2):
        row = v0[l, pl.ds(4 + d // 8, 1), :]
        ub[l:l + 1, :] = pltpu.roll(jnp.broadcast_to(row, (8, D)), lax.rem(D - 96 * lax.rem(d, 8), D), 1)[0:1, :96]
        tab[:, l, :] = v3[16 * l:16 * l + H, :NB]
    for cp in last:
        cp.wait()


def run_unpack(*args):
    V = pl.BlockSpec(memory_space=pltpu.VMEM)
    ANY = pl.BlockSpec(memory_space=pl.ANY)
    sds = jax.ShapeDtypeStruct
    w = sds((2, 24), F32)
    outs = (sds((R, D), BF16), sds((R, D), BF16), w, w, sds((2, 24, 2304), F32), w, w, sds((H, 2, NB), F32), sds((2, 24, D), F32), w, w, w, w,
            sds((2, 24, FF), F32), sds((2, 96), F32), sds((2, 96, D), F32), w, w)
    vm = pltpu.VMEM
    return pl.pallas_call(
        unpack, out_shape=outs, in_specs=[ANY] * 6, out_specs=(ANY, ANY) + (V,) * 16, name="unpack",
        scratch_shapes=[vm((4, 288, 384), BF16), vm((4, 8, D), F32), vm((2, D), F32), vm((32, 128), F32), vm((R, D), BF16), vm((R, D), BF16), pltpu.SemaphoreType.DMA((8,))],
        compiler_params=pltpu.CompilerParams(vmem_limit_bytes=63400000))(*args)


def body(*args):
    so, go, *outs = run_unpack(*run_chain(*args)[:6])
    outs[5] = jnp.transpose(outs[5], (1, 0, 2))
    return (so.reshape(1, 2, MB, D), go.reshape(1, 2, MB, D)) + tuple(outs)


def solution(mesh):
    data, whole = P("dp", None, None), P()
    w1, w2 = P(None, "dp"), P(None, "dp", None)
    return jax.shard_map(
        body,
        mesh=mesh,
        in_specs=(data, data, P("dp", None)) + (whole,) * 17,
        out_specs=(P("section", "dp", None, None),) * 2 + (w1, w1, w2, w1, w1, P(), w2, w1, w1, w1, w1, w2, w1, w2, w1, w1),
        check_vma=False,
    )
```
